1024 devices in a mesh: ep: 64 (over y_lo, z), dp: 16 (over y_hi, x, core).
Axes of the slice: x: 4, y: 8 (y_hi: 2, y_lo: 4; y = y_hi * 4 + y_lo), z: 16, core: 2. Of those that a mesh axis runs over, the one named last changes fastest.
Arguments:
- tokens_first: bfloat16 [131072, 2048], P(('ep', 'dp')), may hold values from -6 to 6
- routes_first: int32 [131072, 1], P(('ep', 'dp')), may hold values from 0 to 63; in each aligned block of 128 rows (0 to 127, 128 to 255, ...) at most 4 rows name the same one
- gates_first: bfloat16 [131072, 1], P(('ep', 'dp')), may hold values from 0.099609375 to 0.5
- gate_up_weight: bfloat16 [64, 2048, 768], P('ep'), may hold values from -0.125 to 0.125
- down_weight: bfloat16 [64, 384, 2048], P('ep'), may hold values from -0.3125 to 0.3125
- saved_inputs: bfloat16 [64, 16, 256, 2048], P('ep', 'dp'), may hold values from -6 to 6
- upstream: bfloat16 [131072, 2048], P(('ep', 'dp')), may hold values from -0.3984375 to 0.3984375
- routes_second: int32 [131072, 1], P(('ep', 'dp')), may hold values from 0 to 63; in each aligned block of 128 rows (0 to 127, 128 to 255, ...) at most 4 rows name the same one
- gates_second: bfloat16 [131072, 1], P(('ep', 'dp')), may hold values from 0.099609375 to 0.5
Outputs:
- mixed_first: bfloat16 [131072, 2048], P(('ep', 'dp'))
- gate_grads: float32 [131072, 1], P(('ep', 'dp'))
- gate_up_grad: bfloat16 [64, 2048, 768], P('ep', 'dp')
- down_grad: bfloat16 [64, 384, 2048], P('ep', None, 'dp')
The draws below stay inside these ranges and needn't reach their ends.
Inputs may be any that keep to these rules, and one draw needn't show every extreme that they name: `routes_first`: each row names 1 different experts; in the rows of one device no expert is named more than 4 times, a bound that some block reaches. `routes_second`: each row names 1 different experts; in the rows of one device no expert is named more than 4 times, a bound that some block reaches.
All inputs are finite; a program needn't handle non-finite values.
Results may differ from the reference program's by a relative error of at most 0.014.
Values may be sent and summed in bfloat16 or wider, within the bound.
No kernel may reach another device: no remote copies, remote signals or barrier semaphores. Data moves between devices by JAX's collectives and lax.ppermute only.
A program may use at most 64 MiB of HBM per device.

```python
import math
import jax
import jax.numpy as jnp
import numpy as np
from jax import lax

D = 2048
HID = 384
TOP = 1
TOK_DEV = 128
EXPERTS = 64
CAP = 4
TOKENS = 131072
N_EP = 64
N_DP = 16


def strengthened(values, own_key, source, target, parts, factor):
    owner, partner = [(jnp.arange(values.shape[dim]) // (values.shape[dim] // parts)).reshape([-1 if axis == dim else 1 for axis in range(values.ndim)]) for dim in (source, target)]
    chosen = jax.random.permutation(own_key, parts)[partner]
    strong = (owner == chosen) | (owner == (partner + parts // 2) % parts)
    return jnp.where(strong, factor * values, values)


def steps_of(own_key, dims, pieces, least, top_value):
    def one(dim, parts):
        draws = jax.random.uniform(jax.random.fold_in(jax.random.fold_in(own_key, 6), dim), (parts,), jnp.float32, least / len(pieces), top_value / len(pieces))
        return jnp.repeat(jnp.exp(draws), dims[dim] // parts).reshape((-1,) + (1,) * (len(dims) - dim - 1))

    level = one(*pieces[0])
    for cut in pieces[1:]:
        level = level * one(*cut)
    return level


def routed_block(rng, own, number, rows, number_of, top, bound, skew):
    order = jax.random.permutation(rng, number_of)
    packed, ordinary = load_shares(number_of, rows * top, bound, skew, True), load_shares(number_of, rows * top, bound, skew, False)
    places = jnp.arange(number_of)

    def named(sizes, offset_by):
        used = int((sizes > 0).sum())
        fixed = max(1, used // 4)
        shifted = fixed + (places - fixed + offset_by * (used - fixed)) % max(1, number_of - fixed)
        return jnp.zeros((number_of,), jnp.int32).at[order[jnp.where(places < fixed, places, shifted)]].set(jnp.asarray(sizes, jnp.int32))

    sizes = jnp.where(number % 4 == 0, named(packed, number // 4), named(ordinary, number - number // 4 - 1))
    mixed = jax.random.permutation(jax.random.fold_in(own, 3), number_of)
    source_of, sink = mixed[0:number_of // 2 * 2:2], mixed[1:number_of // 2 * 2:2]
    margin = jnp.minimum(sizes[source_of] - 1, bound - sizes[sink]) // 2
    margin = jnp.where((source_of == order[0]) | (sink == order[0]) | (sizes[sink] == 0), 0, jnp.maximum(margin, 0))
    shifted = jax.random.randint(jax.random.fold_in(own, 4), (number_of // 2,), 0, 1 << 20) % (margin + 1)
    sizes = sizes.at[source_of].add(-shifted).at[sink].add(shifted)
    members = jnp.searchsorted(jnp.cumsum(sizes), jnp.arange(rows * top), side="right").astype(jnp.int32)
    grid = members.reshape(top, rows).T
    grid = grid[jax.random.permutation(jax.random.fold_in(own, 1), rows)]
    offset_by = jax.random.randint(jax.random.fold_in(own, 2), (rows, 1), 0, top)
    return jnp.take_along_axis(grid, (jnp.arange(top)[None, :] + offset_by) % top, axis=1)


def load_shares(count, total, reach, slope, full):
    weights = [(1 << 20) // math.isqrt(grade ** slope) + 1 for grade in range(1, count + 1)]
    largest = reach if full else min(reach, max(-(-total // count), total * weights[0] // sum(weights)))
    least = 1 if total - largest >= count - 1 else 0
    holding, rest = [largest] + [least] * (count - 1), total - largest - least * (count - 1)
    while rest > 0:
        free = [i for i in range(1, count) if holding[i] < largest] or [i for i in range(1, count) if holding[i] < reach]
        whole, remaining = sum([weights[i] for i in free]), rest
        for i in free:
            addition = min(reach - holding[i], max(1, remaining * weights[i] // whole), rest)
            holding[i] = holding[i] + addition
            rest = rest - addition
    return np.array(holding)


def normal_values(own_key, extent, deviation, reach, split=(), kind=jnp.bfloat16):
    values = jax.random.normal(own_key, extent, jnp.float32) * deviation
    if len(split) > 0:
        values = steps_of(own_key, extent, split, -0.22, 0.18) * values
    return jnp.clip(values, min=-reach, max=reach).astype(kind)


def heavy_noise(stream_key, dims, scale, reach, cuts, heavy, kind=jnp.bfloat16):
    values = scale * jax.random.normal(stream_key, dims, jnp.float32)
    if cuts:
        values = values * steps_of(stream_key, dims, cuts, -0.22, 0.18)
    return jnp.clip(strengthened(values, jax.random.fold_in(stream_key, 3), *heavy), -reach, reach).astype(kind)


def setup_inputs(seed: int = 0) -> dict:
    key_list = jax.random.split(jax.random.key(seed), 10)
    tokens_first = normal_values(key_list[0], (TOKENS, D), 1.0, 6.0, ((0, 1024),))
    routes_first_keys = jax.random.split(jax.random.fold_in(key_list[1], 1), TOKENS // TOK_DEV)
    routes_first_turns = jax.random.permutation(jax.random.fold_in(key_list[1], 3), TOKENS // TOK_DEV)
    routes_first = jax.vmap(lambda own, number: routed_block(jax.random.fold_in(key_list[1], 2), own, number, TOK_DEV, EXPERTS, TOP, CAP, 2))(routes_first_keys, routes_first_turns).reshape((TOKENS, TOP))
    gates_first = jnp.clip(0.099609375 + 0.40039062 * jax.random.uniform(key_list[2], (TOKENS, TOP), jnp.float32) ** steps_of(key_list[2], (TOKENS, TOP), ((0, 1024),), -0.2, 0.2), 0.099609375, 0.5).astype(jnp.bfloat16)
    gate_up_weight = normal_values(key_list[3], (EXPERTS, D, 2 * HID), D ** -0.5, 0.125, ((0, 64),))
    down_weight = normal_values(key_list[4], (EXPERTS, HID, D), HID ** -0.5, 0.3125, ((0, 64),))
    saved_inputs = heavy_noise(key_list[5], (EXPERTS, N_DP, N_EP * CAP, D), 1.0, 6.0, ((0, 64), (1, 16)), (1, 3, 16, 2.0))
    upstream = normal_values(key_list[6], (TOKENS, D), 0.05, 0.3984375, ((0, 1024),))
    routes_second_keys = jax.random.split(jax.random.fold_in(key_list[7], 1), TOKENS // TOK_DEV)
    routes_second_turns = jax.random.permutation(jax.random.fold_in(key_list[7], 3), TOKENS // TOK_DEV)
    routes_second = jax.vmap(lambda own, number: routed_block(jax.random.fold_in(key_list[7], 2), own, number, TOK_DEV, EXPERTS, TOP, CAP, 2))(routes_second_keys, routes_second_turns).reshape((TOKENS, TOP))
    gates_second = jnp.clip(0.099609375 + 0.40039062 * jax.random.uniform(key_list[8], (TOKENS, TOP), jnp.float32) ** steps_of(key_list[8], (TOKENS, TOP), ((0, 1024),), -0.2, 0.2), 0.099609375, 0.5).astype(jnp.bfloat16)
    return {"tokens_first": tokens_first, "routes_first": routes_first, "gates_first": gates_first, "gate_up_weight": gate_up_weight, "down_weight": down_weight, "saved_inputs": saved_inputs, "upstream": upstream, "routes_second": routes_second, "gates_second": gates_second}


def slot_index(routing):
    expert_ids = jnp.arange(EXPERTS, dtype=jnp.int32)
    onehot = (routing[:, :, None] == expert_ids).astype(jnp.int32)
    counts = jnp.sum(onehot, axis=1)
    before = jnp.cumsum(counts, axis=0) - counts
    return jnp.sum(onehot * before[:, None, :], axis=2).astype(jnp.int32)


def reference(tokens_first, routes_first, gates_first, gate_up_weight, down_weight, saved_inputs, upstream, routes_second, gates_second):
    devices = N_EP * N_DP
    highest = lax.Precision.HIGHEST
    first_float = tokens_first.reshape(devices, TOK_DEV, D).astype(jnp.float32)
    first_routes = routes_first.reshape(devices, TOK_DEV, TOP)
    first_gates = gates_first.reshape(devices, TOK_DEV, TOP).astype(jnp.float32)
    first_slots = jax.vmap(slot_index)(first_routes)
    upstream_float = upstream.reshape(devices, TOK_DEV, D).astype(jnp.float32)
    second_routes = routes_second.reshape(devices, TOK_DEV, TOP)
    second_gates = gates_second.reshape(devices, TOK_DEV, TOP).astype(jnp.float32)
    second_slots = jax.vmap(slot_index)(second_routes)
    slot_ids = jnp.arange(CAP, dtype=jnp.int32)

    def hits(routing, slots, expert_id):
        return ((routing == expert_id)[..., None] & (slots[..., None] == slot_ids)).astype(jnp.float32)

    def regroup(values):
        shaped = values.reshape((N_EP, N_DP, CAP) + values.shape[2:])
        return jnp.swapaxes(shaped, 0, 1).reshape((N_DP * N_EP * CAP,) + values.shape[2:])

    def per_expert(carry, expert_id):
        mixed_sum, gate_sum = carry
        weight_gu = gate_up_weight[expert_id]
        weight_down = down_weight[expert_id]
        hit_first = hits(first_routes, first_slots, expert_id)
        slot_rows = jnp.einsum("ntc,ntd->ncd", jnp.sum(hit_first, axis=2), first_float, precision=highest).astype(jnp.bfloat16)
        projected = jnp.dot(slot_rows.reshape(-1, D), weight_gu, preferred_element_type=jnp.float32)
        activated = (jax.nn.silu(projected[:, :HID]) * projected[:, HID:]).astype(jnp.bfloat16)
        expert_out = jnp.dot(activated, weight_down, preferred_element_type=jnp.float32).astype(jnp.bfloat16)
        expert_out = expert_out.reshape(devices, CAP, D).astype(jnp.float32)
        token_weight = jnp.einsum("ntkc,ntk->ntc", hit_first, first_gates, precision=highest)
        mixed_sum = mixed_sum + jnp.einsum("ntc,ncd->ntd", token_weight, expert_out, precision=highest)

        hit_second = hits(second_routes, second_slots, expert_id)
        grad_slots = jnp.einsum("ntc,ntd->ncd", jnp.sum(hit_second, axis=2), upstream_float, precision=highest).astype(jnp.bfloat16)
        slot_gates = jnp.einsum("ntkc,ntk->nc", hit_second, second_gates, precision=highest)
        grad_group = regroup(grad_slots)
        gate_group = regroup(slot_gates).reshape(-1, 1)
        saved_rows = saved_inputs[expert_id].reshape(-1, D)
        projected_b = jnp.dot(saved_rows, weight_gu, preferred_element_type=jnp.float32)
        gate_part = projected_b[:, :HID]
        up_part = projected_b[:, HID:]
        squash = jax.nn.sigmoid(gate_part)
        swish = jax.nn.silu(gate_part)
        activated_b = (swish * up_part).astype(jnp.bfloat16)
        grad_hidden = lax.dot_general(grad_group, weight_down, (((1,), (1,)), ((), ())), preferred_element_type=jnp.float32)
        slot_value = jnp.sum(grad_hidden * activated_b.astype(jnp.float32), axis=1)
        slot_back = jnp.swapaxes(slot_value.reshape(N_DP, N_EP, CAP), 0, 1).reshape(devices, CAP)
        gate_sum = gate_sum + jnp.einsum("ntkc,nc->ntk", hit_second, slot_back, precision=highest)
        grad_scaled = gate_group * grad_hidden
        grad_gate = grad_scaled * up_part * squash * (1.0 + gate_part * (1.0 - squash))
        grad_up = grad_scaled * swish
        grad_both = jnp.concatenate([grad_gate, grad_up], axis=1).astype(jnp.bfloat16)
        grad_rows = (gate_group * grad_group.astype(jnp.float32)).astype(jnp.bfloat16)
        group_inputs = saved_rows.reshape(N_DP, -1, D).astype(jnp.float32)
        term_gu = jnp.einsum("nrd,nrj->ndj", group_inputs, grad_both.reshape(N_DP, -1, 2 * HID).astype(jnp.float32), precision=highest).astype(jnp.bfloat16)
        grad_gu = jnp.sum(term_gu.astype(jnp.float32), axis=0).astype(jnp.bfloat16)
        term_down = jnp.einsum("nrh,nrd->nhd", activated_b.reshape(N_DP, -1, HID).astype(jnp.float32), grad_rows.reshape(N_DP, -1, D).astype(jnp.float32), precision=highest).astype(jnp.bfloat16)
        grad_dn = jnp.sum(term_down.astype(jnp.float32), axis=0).astype(jnp.bfloat16)
        return (mixed_sum, gate_sum), (grad_gu, grad_dn)

    start = (jnp.zeros((devices, TOK_DEV, D), jnp.float32), jnp.zeros((devices, TOK_DEV, TOP), jnp.float32))
    (mixed_sum, gate_sum), (gu_all, down_all) = lax.scan(per_expert, start, jnp.arange(EXPERTS, dtype=jnp.int32))
    return (mixed_sum.reshape(TOKENS, D).astype(jnp.bfloat16), gate_sum.reshape(TOKENS, TOP), gu_all, down_all)
```

```python
import functools

import jax
import jax.numpy as jnp
from jax import lax
from jax.experimental import pallas as pl
from jax.experimental.pallas import tpu as pltpu
from jax.sharding import Mesh, PartitionSpec as P

BF16 = jnp.bfloat16
F32 = jnp.float32
I32 = jnp.int32
EP = ("yl", "z")
ALL = ("yl", "z", "yh", "x", "core")
CHUNK = 16


def iota(shape, dim):
    return lax.broadcasted_iota(I32, shape, dim)


def dot(a, b, ca=1, cb=0):
    return lax.dot_general(a, b, (((ca,), (cb,)), ((), ())), preferred_element_type=F32)


def slots_of(routes, experts):
    tokens = routes.shape[1]
    onehot = (iota((experts, tokens), 0) == routes).astype(F32)
    earlier = (iota((tokens, tokens), 0) < iota((tokens, tokens), 1)).astype(F32)
    before = dot(onehot.astype(BF16), earlier.astype(BF16))
    return onehot, jnp.sum(onehot * before, axis=0, keepdims=True).astype(I32)


def order_of(rows, cap, dim):
    j = iota((rows, rows), dim)
    pieces = CHUNK // cap
    per = rows // pieces
    return (j % CHUNK) // cap * per + j // CHUNK * cap + j % cap


def gather_order(rows, cap):
    return (iota((rows, rows), 0) == order_of(rows, cap, 1)).astype(F32).astype(BF16)


def scatter_order(rows, cap):
    return (iota((rows, rows), 1) == order_of(rows, cap, 0)).astype(F32).astype(BF16)


GROUP = 256


def from_chunks(chunks_ref, rows_ref, cap):
    width = chunks_ref.shape[1]
    pieces = CHUNK // cap
    per = GROUP // pieces
    order = gather_order(GROUP, cap)
    for g in range(chunks_ref.shape[0] // GROUP):
        part = dot(order, chunks_ref[g * GROUP : (g + 1) * GROUP, :]).astype(BF16)
        for q in range(pieces):
            rows_ref[g * per : (g + 1) * per, q * width : (q + 1) * width] = part[
                q * per : (q + 1) * per
            ]


def to_chunks(rows_ref, chunks_ref, cap):
    width = chunks_ref.shape[1]
    pieces = CHUNK // cap
    per = GROUP // pieces
    order = scatter_order(GROUP, cap)
    for g in range(chunks_ref.shape[0] // GROUP):
        part = jnp.concatenate(
            [
                rows_ref[g * per : (g + 1) * per, q * width : (q + 1) * width]
                for q in range(pieces)
            ],
            axis=0,
        )
        chunks_ref[g * GROUP : (g + 1) * GROUP, :] = dot(order, part).astype(BF16)


def send_rows(experts, cap, routes, weights, tokens_ref, chunks_ref):
    tokens = routes.shape[1]
    width = chunks_ref.shape[1]
    _, slots = slots_of(routes, experts)
    base = routes * CHUNK + slots
    for g in range(chunks_ref.shape[0] // GROUP):
        row = iota((GROUP, tokens), 0) + g * GROUP
        total = None
        for q in range(CHUNK // cap):
            select = jnp.where(row == base + q * cap, weights, 0.0).astype(BF16)
            term = dot(select, tokens_ref[:, q * width : (q + 1) * width])
            total = term if total is None else total + term
        chunks_ref[g * GROUP : (g + 1) * GROUP, :] = total.astype(BF16)
    return slots


def dispatch_second_kernel(experts, cap, routes_ref, gates_ref, tokens_ref, chunks_ref):
    send_rows(
        experts, cap, routes_ref[...], gates_ref[...].astype(F32), tokens_ref, chunks_ref
    )


def dispatch_first_kernel(
    experts, cap, routes_ref, gates_ref, tokens_ref, chunks_ref, mix_ref
):
    routes = routes_ref[...]
    slots = send_rows(
        experts, cap, routes, jnp.ones(routes.shape, F32), tokens_ref, chunks_ref
    )
    places = experts * cap
    hit = iota((places, routes.shape[1]), 0) == routes * cap + slots
    mix_ref[...] = jnp.where(hit, gates_ref[...].astype(F32), 0.0).T.astype(BF16)


def saved_kernel(x_ref, gu_ref, act_ref, gate_ref, up_ref):
    hid = act_ref.shape[1]
    both = dot(x_ref[...], gu_ref[...])
    gate, up = both[:, :hid], both[:, hid:]
    squash = jax.nn.sigmoid(gate)
    swish = gate * squash
    act_ref[...] = (swish * up).astype(BF16)
    gate_ref[...] = up * squash * (1.0 + gate * (1.0 - squash))
    up_ref[...] = swish


def backward_kernel(
    cap,
    at_ref,
    chunks_ref,
    down_ref,
    x_ref,
    act_ref,
    gate_ref,
    up_ref,
    keep_ref,
    send_ref,
    value_ref,
    rows_ref,
    both_ref,
):
    hid = act_ref.shape[1]
    block = keep_ref.shape[1]
    from_chunks(chunks_ref, rows_ref, cap)
    scaled = dot(rows_ref[...], down_ref[...], 1, 1)
    product = scaled * act_ref[...].astype(F32)
    folded = product[:, :128]
    for k in range(1, hid // 128):
        folded = folded + product[:, k * 128 : (k + 1) * 128]
    value_ref[...] = jnp.sum(folded.T, axis=0, keepdims=True)
    both_ref[:, :hid] = (scaled * gate_ref[...]).astype(BF16)
    both_ref[:, hid:] = (scaled * up_ref[...]).astype(BF16)
    y, x, core = at_ref[0], at_ref[1], at_ref[2]
    n_x = keep_ref.shape[0] // 2
    for out_ref, other in ((send_ref, 1), (keep_ref, 0)):
        for n in range(2 * n_x):
            to = ((y + n % 2) % 2 * n_x + (x + n // 2) % n_x) * 2 + (core + other) % 2
            columns = pl.ds(pl.multiple_of(to * block, block), block)
            out_ref[n, :, : 2 * hid] = dot(x_ref[:, columns], both_ref[...], 0, 0).astype(BF16)
            out_ref[n, :, 2 * hid :] = dot(rows_ref[:, columns], act_ref[...], 0, 0).astype(BF16)


def forward_kernel(cap, chunks_ref, gu_ref, down_ref, out_ref, rows_ref):
    hid = down_ref.shape[0]
    from_chunks(chunks_ref, rows_ref, cap)
    both = dot(rows_ref[...], gu_ref[...])
    act = (jax.nn.silu(both[:, :hid]) * both[:, hid:]).astype(BF16)
    rows_ref[...] = dot(act, down_ref[...]).astype(BF16)
    to_chunks(rows_ref, out_ref, cap)


def combine_kernel(cap, chunks_ref, mix_ref, out_ref, rows_ref):
    from_chunks(chunks_ref, rows_ref, cap)
    out_ref[...] = dot(mix_ref[...], rows_ref[...]).astype(BF16)


def gate_grad_kernel(cap, at_ref, values_ref, routes_ref, gates_ref, out_ref):
    values = values_ref[...]
    experts, places = values.shape
    onehot, slots = slots_of(routes_ref[...], experts)
    lane = iota((experts, places), 1)
    total = jnp.zeros(out_ref.shape, F32)
    for c in range(cap):
        mine = jnp.sum(
            jnp.where(lane == at_ref[0] * cap + c, values, 0.0), axis=1, keepdims=True
        )
        here = jnp.sum(onehot * mine, axis=0, keepdims=True)
        total = total + jnp.where(slots == c, here, 0.0)
    out_ref[...] = total / gates_ref[...].astype(F32)


def add_kernel(*refs):
    *terms, out_ref = refs
    total = terms[0][...].astype(F32)
    for term in terms[1:]:
        total = total + term[...].astype(F32)
    out_ref[...] = total.astype(BF16)


def finish_kernel(hid, a_ref, b_ref, gu_ref, down_ref):
    total = a_ref[...].astype(F32) + b_ref[...].astype(F32)
    gu_ref[...] = total[:, : 2 * hid].astype(BF16)
    down_ref[...] = total[:, 2 * hid :].T.astype(BF16)


VMEM = pl.BlockSpec(memory_space=pltpu.VMEM)
SMEM = pl.BlockSpec(memory_space=pltpu.SMEM)


def call(kernel, name, outs, args, scratch=(), scalars=0, flops=0, moved=0):
    shapes = [jax.ShapeDtypeStruct(*o) for o in outs]
    result = pl.pallas_call(
        kernel,
        name=name,
        out_shape=shapes,
        in_specs=[SMEM] * scalars + [VMEM] * (len(args) - scalars),
        out_specs=[VMEM] * len(outs),
        scratch_shapes=[pltpu.VMEM(*s) for s in scratch],
        compiler_params=pltpu.CompilerParams(vmem_limit_bytes=40 * 2**20),
        cost_estimate=pl.CostEstimate(flops=flops, bytes_accessed=moved, transcendentals=0),
    )(*args)
    return result[0] if len(outs) == 1 else result


def local(
    n_x,
    tokens_first,
    routes_first,
    gates_first,
    gate_up_weight,
    down_weight,
    saved_inputs,
    upstream,
    routes_second,
    gates_second,
):
    experts = lax.axis_size("yl") * lax.axis_size("z")
    places, model = saved_inputs.shape[2:]
    cap = places // experts
    tokens = tokens_first.shape[0]
    width = model * cap // CHUNK
    gu, down, x = gate_up_weight[0], down_weight[0], saved_inputs[0, 0]
    hid = down.shape[0]
    block = model // (4 * n_x)
    MB = 2**20

    def row(a):
        return a.reshape(1, tokens)

    def exchange(chunks):
        chunks = chunks.reshape(experts, CHUNK, width)
        moved = lax.all_to_all(chunks, EP, split_axis=0, concat_axis=0, tiled=True)
        return moved.reshape(experts * CHUNK, width)

    chunk_shape = ((experts * CHUNK, width), BF16)
    row_shape = ((places, model), BF16)
    here = jnp.stack(
        [lax.axis_index("yh"), lax.axis_index("x"), lax.axis_index("core")]
    ).astype(I32)
    home = lax.axis_index(EP).astype(I32).reshape(1)

    send_second = call(
        functools.partial(dispatch_second_kernel, experts, cap),
        "dispatch_second",
        [chunk_shape],
        (row(routes_second), row(gates_second), upstream),
        flops=2**29,
        moved=2 * MB,
    )
    got_second = exchange(send_second)
    send_first, mix = call(
        functools.partial(dispatch_first_kernel, experts, cap),
        "dispatch_first",
        [chunk_shape, ((tokens, places), BF16)],
        (row(routes_first), row(gates_first), tokens_first),
        flops=2**29,
        moved=2 * MB,
    )
    act, by_gate, by_up = call(
        saved_kernel,
        "saved",
        [((places, hid), BF16), ((places, hid), F32), ((places, hid), F32)],
        (x, gu),
        flops=2**30,
        moved=6 * MB,
    )
    got_first = exchange(send_first)

    half = ((2 * n_x, block, 3 * hid), BF16)
    keep, send, value = call(
        functools.partial(backward_kernel, cap),
        "backward",
        [half, half, ((1, places), F32)],
        (here, got_second, down, x, act, by_gate, by_up),
        scratch=(row_shape, ((places, 2 * hid), BF16)),
        scalars=1,
        flops=2**31,
        moved=12 * MB,
    )
    values = lax.all_gather(value.reshape(places), EP)
    other = lax.ppermute(send, "core", [(0, 1), (1, 0)])
    pair = ((2, block, 3 * hid), BF16)

    def add(*terms):
        return call(add_kernel, "add", [(terms[0].shape, BF16)], terms, moved=len(terms) * MB)

    def summed(k):
        return add(keep[2 * k : 2 * k + 2], other[2 * k : 2 * k + 2])

    terms = [summed(0)]
    for k in range(1, n_x):
        terms.append(
            lax.ppermute(summed(k), "x", [(i, (i + k) % n_x) for i in range(n_x)])
        )
    quarter = add(*terms)
    far = lax.ppermute(quarter[1], "yh", [(0, 1), (1, 0)])
    gate_up_grad, down_grad = call(
        functools.partial(finish_kernel, hid),
        "finish",
        [((block, 2 * hid), BF16), ((hid, block), BF16)],
        (quarter[0], far),
        moved=MB,
    )
    gate_grads = call(
        functools.partial(gate_grad_kernel, cap),
        "gate_grad",
        [((1, tokens), F32)],
        (home, values, row(routes_second), row(gates_second)),
        scalars=1,
        moved=MB // 8,
    )

    send_back = call(
        functools.partial(forward_kernel, cap),
        "forward",
        [chunk_shape],
        (got_first, gu, down),
        scratch=(row_shape,),
        flops=2**31,
        moved=7 * MB,
    )
    got_back = exchange(send_back)
    mixed_first = call(
        functools.partial(combine_kernel, cap),
        "combine",
        [((tokens, model), BF16)],
        (got_back, mix),
        scratch=(row_shape,),
        flops=2**29,
        moved=2 * MB,
    )
    return (
        mixed_first,
        gate_grads.reshape(tokens, 1),
        gate_up_grad[None],
        down_grad[None],
    )


def solution(mesh):
    n_ep, n_dp = mesh.devices.shape
    lows = 4
    n_x = n_dp // 4
    fine = Mesh(mesh.devices.reshape(lows, n_ep // lows, 2, n_x, 2), ALL)
    tokens = P(ALL, None)
    return jax.shard_map(
        functools.partial(local, n_x),
        mesh=fine,
        in_specs=(
            tokens,
            tokens,
            tokens,
            P(EP, None, None),
            P(EP, None, None),
            P(EP, ("yh", "x", "core"), None, None),
            tokens,
            tokens,
            tokens,
        ),
        out_specs=(
            tokens,
            tokens,
            P(EP, ("yh", "x", "core"), None),
            P(EP, None, ("yh", "x", "core")),
        ),
        check_vma=False,
    )
```

```python
import functools

import jax
import jax.numpy as jnp
from jax import lax
from jax.experimental import pallas as pl
from jax.experimental.pallas import tpu as pltpu
from jax.sharding import Mesh, PartitionSpec as P

BF16 = jnp.bfloat16
F32 = jnp.float32
I32 = jnp.int32
EP = ("yl", "z")
ALL = ("yl", "z", "yh", "x", "core")
CHUNK = 16


def iota(shape, dim):
    return lax.broadcasted_iota(I32, shape, dim)


def dot(a, b, ca=1, cb=0):
    return lax.dot_general(a, b, (((ca,), (cb,)), ((), ())), preferred_element_type=F32)


def slots_of(routes, experts):
    tokens = routes.shape[1]
    onehot = (iota((experts, tokens), 0) == routes).astype(F32)
    earlier = (iota((tokens, tokens), 0) < iota((tokens, tokens), 1)).astype(F32)
    before = dot(onehot.astype(BF16), earlier.astype(BF16))
    return onehot, jnp.sum(onehot * before, axis=0, keepdims=True).astype(I32)


def order_of(rows, cap, dim):
    j = iota((rows, rows), dim)
    pieces = CHUNK // cap
    per = rows // pieces
    return (j % CHUNK) // cap * per + j // CHUNK * cap + j % cap


def gather_order(rows, cap):
    return (iota((rows, rows), 0) == order_of(rows, cap, 1)).astype(F32).astype(BF16)


def scatter_order(rows, cap):
    return (iota((rows, rows), 1) == order_of(rows, cap, 0)).astype(F32).astype(BF16)


GROUP = 256


def from_chunks(chunks_ref, rows_ref, cap):
    width = chunks_ref.shape[1]
    pieces = CHUNK // cap
    per = GROUP // pieces
    order = gather_order(GROUP, cap)
    for g in range(chunks_ref.shape[0] // GROUP):
        part = dot(order, chunks_ref[g * GROUP : (g + 1) * GROUP, :]).astype(BF16)
        for q in range(pieces):
            rows_ref[g * per : (g + 1) * per, q * width : (q + 1) * width] = part[
                q * per : (q + 1) * per
            ]


def to_chunks(rows_ref, chunks_ref, cap):
    width = chunks_ref.shape[1]
    pieces = CHUNK // cap
    per = GROUP // pieces
    order = scatter_order(GROUP, cap)
    for g in range(chunks_ref.shape[0] // GROUP):
        part = jnp.concatenate(
            [
                rows_ref[g * per : (g + 1) * per, q * width : (q + 1) * width]
                for q in range(pieces)
            ],
            axis=0,
        )
        chunks_ref[g * GROUP : (g + 1) * GROUP, :] = dot(order, part).astype(BF16)


def send_rows(experts, cap, routes, weights, tokens_ref, chunks_ref):
    tokens = routes.shape[1]
    width = chunks_ref.shape[1]
    _, slots = slots_of(routes, experts)
    base = routes * CHUNK + slots
    for g in range(chunks_ref.shape[0] // GROUP):
        row = iota((GROUP, tokens), 0) + g * GROUP
        total = None
        for q in range(CHUNK // cap):
            select = jnp.where(row == base + q * cap, weights, 0.0).astype(BF16)
            term = dot(select, tokens_ref[:, q * width : (q + 1) * width])
            total = term if total is None else total + term
        chunks_ref[g * GROUP : (g + 1) * GROUP, :] = total.astype(BF16)
    return slots


def dispatch_second_kernel(experts, cap, routes_ref, gates_ref, tokens_ref, chunks_ref):
    send_rows(
        experts, cap, routes_ref[...], gates_ref[...].astype(F32), tokens_ref, chunks_ref
    )


def dispatch_first_kernel(
    experts, cap, routes_ref, gates_ref, tokens_ref, chunks_ref, mix_ref
):
    routes = routes_ref[...]
    slots = send_rows(
        experts, cap, routes, jnp.ones(routes.shape, F32), tokens_ref, chunks_ref
    )
    places = experts * cap
    hit = iota((places, routes.shape[1]), 0) == routes * cap + slots
    mix_ref[...] = jnp.where(hit, gates_ref[...].astype(F32), 0.0).T.astype(BF16)


def saved_kernel(x_ref, gu_ref, act_ref, gate_ref, up_ref):
    hid = act_ref.shape[1]
    both = dot(x_ref[...], gu_ref[...])
    gate, up = both[:, :hid], both[:, hid:]
    squash = jax.nn.sigmoid(gate)
    swish = gate * squash
    act_ref[...] = (swish * up).astype(BF16)
    gate_ref[...] = up * squash * (1.0 + gate * (1.0 - squash))
    up_ref[...] = swish


def backward_kernel(
    cap,
    at_ref,
    chunks_ref,
    down_ref,
    x_ref,
    act_ref,
    gate_ref,
    up_ref,
    keep_ref,
    send_ref,
    value_ref,
    rows_ref,
    both_ref,
):
    hid = act_ref.shape[1]
    block = keep_ref.shape[1]
    from_chunks(chunks_ref, rows_ref, cap)
    scaled = dot(rows_ref[...], down_ref[...], 1, 1)
    product = scaled * act_ref[...].astype(F32)
    folded = product[:, :128]
    for k in range(1, hid // 128):
        folded = folded + product[:, k * 128 : (k + 1) * 128]
    value_ref[...] = jnp.sum(folded.T, axis=0, keepdims=True)
    both_ref[:, :hid] = (scaled * gate_ref[...]).astype(BF16)
    both_ref[:, hid:] = (scaled * up_ref[...]).astype(BF16)
    y, x, core = at_ref[0], at_ref[1], at_ref[2]
    n_x = keep_ref.shape[0] // 2
    for out_ref, other in ((send_ref, 1), (keep_ref, 0)):
        for n in range(2 * n_x):
            to = ((y + n % 2) % 2 * n_x + (x + n // 2) % n_x) * 2 + (core + other) % 2
            columns = pl.ds(pl.multiple_of(to * block, block), block)
            out_ref[n, :, : 2 * hid] = dot(x_ref[:, columns], both_ref[...], 0, 0).astype(BF16)
            out_ref[n, :, 2 * hid :] = dot(rows_ref[:, columns], act_ref[...], 0, 0).astype(BF16)


def forward_kernel(cap, chunks_ref, gu_ref, down_ref, *refs):
    out_ref, rows_ref = refs[-2:]
    hid = down_ref.shape[0]
    from_chunks(chunks_ref, rows_ref, cap)
    both = dot(rows_ref[...], gu_ref[...])
    act = (jax.nn.silu(both[:, :hid]) * both[:, hid:]).astype(BF16)
    rows_ref[...] = dot(act, down_ref[...]).astype(BF16)
    to_chunks(rows_ref, out_ref, cap)


def combine_kernel(cap, chunks_ref, mix_ref, out_ref, rows_ref):
    from_chunks(chunks_ref, rows_ref, cap)
    out_ref[...] = dot(mix_ref[...], rows_ref[...]).astype(BF16)


def gate_grad_kernel(cap, digits, at_ref, *refs):
    *value_refs, routes_ref, gates_ref, out_ref = refs
    n_yl, n_high, n_low = digits
    values = jnp.concatenate([ref[...] for ref in value_refs], axis=0)
    experts, places = values.shape
    tokens = out_ref.shape[1]
    routes = routes_ref[...]
    _, slots = slots_of(routes, experts)
    yl, high, low = at_ref[0], at_ref[1] // n_low, at_ref[1] % n_low
    home = yl * (n_high * n_low) + at_ref[1]
    far_yl = (yl + n_yl - routes // (n_high * n_low)) % n_yl
    far_high = (high + n_high - routes // n_low % n_high) % n_high
    far_low = (low + n_low - routes % n_low) % n_low
    source = (far_low * n_high + far_high) * n_yl + far_yl
    hit = (iota((experts, tokens), 0) == source).astype(F32)
    lane = iota((experts, places), 1)
    total = jnp.zeros(out_ref.shape, F32)
    for c in range(cap):
        mine = jnp.sum(jnp.where(lane == home * cap + c, values, 0.0), axis=1, keepdims=True)
        here = jnp.sum(hit * mine, axis=0, keepdims=True)
        total = total + jnp.where(slots == c, here, 0.0)
    out_ref[...] = total / gates_ref[...].astype(F32)


def pair_kernel(a_ref, b_ref, *out_refs):
    for k, out_ref in enumerate(out_refs):
        total = a_ref[2 * k : 2 * k + 2].astype(F32) + b_ref[2 * k : 2 * k + 2].astype(F32)
        out_ref[...] = total.astype(BF16)


def sum_kernel(*refs):
    *terms, near_ref, far_ref = refs
    for k, out_ref in ((1, far_ref), (0, near_ref)):
        total = terms[0][k].astype(F32)
        for term in terms[1:]:
            total = total + term[k].astype(F32)
        out_ref[...] = total.astype(BF16)


def finish_kernel(hid, a_ref, b_ref, gu_ref, down_ref):
    total = a_ref[...].astype(F32) + b_ref[...].astype(F32)
    gu_ref[...] = total[:, : 2 * hid].astype(BF16)
    down_ref[...] = total[:, 2 * hid :].T.astype(BF16)


VMEM = pl.BlockSpec(memory_space=pltpu.VMEM)
SMEM = pl.BlockSpec(memory_space=pltpu.SMEM)
ANY = pl.BlockSpec(memory_space=pl.ANY)


def call(kernel, name, outs, args, scratch=(), scalars=0, after=(), flops=0, moved=0):
    shapes = [jax.ShapeDtypeStruct(*o) for o in outs]
    result = pl.pallas_call(
        kernel,
        name=name,
        out_shape=shapes,
        in_specs=[SMEM] * scalars + [VMEM] * (len(args) - scalars) + [ANY] * len(after),
        out_specs=[VMEM] * len(outs),
        scratch_shapes=[pltpu.VMEM(*s) for s in scratch],
        compiler_params=pltpu.CompilerParams(vmem_limit_bytes=24 * 2**20),
        cost_estimate=pl.CostEstimate(flops=flops, bytes_accessed=moved, transcendentals=0),
    )(*args, *after)
    return result[0] if len(outs) == 1 else result


def local(
    n_x,
    tokens_first,
    routes_first,
    gates_first,
    gate_up_weight,
    down_weight,
    saved_inputs,
    upstream,
    routes_second,
    gates_second,
):
    experts = lax.axis_size("yl") * lax.axis_size("z")
    places, model = saved_inputs.shape[2:]
    cap = places // experts
    tokens = tokens_first.shape[0]
    width = model * cap // CHUNK
    gu, down, x = gate_up_weight[0], down_weight[0], saved_inputs[0, 0]
    hid = down.shape[0]
    block = model // (4 * n_x)
    MB = 2**20

    def row(a):
        return a.reshape(1, tokens)

    def exchange(chunks):
        chunks = chunks.reshape(experts, CHUNK, width)
        moved = lax.all_to_all(chunks, EP, split_axis=0, concat_axis=0, tiled=True)
        return moved.reshape(experts * CHUNK, width)

    chunk_shape = ((experts * CHUNK, width), BF16)
    row_shape = ((places, model), BF16)
    here = jnp.stack(
        [lax.axis_index("yh"), lax.axis_index("x"), lax.axis_index("core")]
    ).astype(I32)
    home = jnp.stack([lax.axis_index("yl"), lax.axis_index("z")]).astype(I32)
    n_yl, n_z = lax.axis_size("yl"), lax.axis_size("z")
    n_high = min(4, n_z)
    n_low = n_z // n_high

    def shifted(a, axis, n, unit, k):
        size = lax.axis_size(axis)
        span = n * unit
        pairs = [(i, i // span * span + (i + k * unit) % span) for i in range(size)]
        return lax.ppermute(a, axis, pairs)

    def spread(a, axis, n, unit):
        return [a] + [shifted(a, axis, n, unit, k) for k in range(1, n)]

    send_second = call(
        functools.partial(dispatch_second_kernel, experts, cap),
        "dispatch_second",
        [chunk_shape],
        (row(routes_second), row(gates_second), upstream),
        flops=2**29,
        moved=2 * MB,
    )
    got_second = exchange(send_second)
    send_first, mix = call(
        functools.partial(dispatch_first_kernel, experts, cap),
        "dispatch_first",
        [chunk_shape, ((tokens, places), BF16)],
        (row(routes_first), row(gates_first), tokens_first),
        flops=2**29,
        moved=2 * MB,
    )
    act, by_gate, by_up = call(
        saved_kernel,
        "saved",
        [((places, hid), BF16), ((places, hid), F32), ((places, hid), F32)],
        (x, gu),
        flops=2**30,
        moved=6 * MB,
    )
    got_first = exchange(send_first)

    half = ((2 * n_x, block, 3 * hid), BF16)
    keep, send, value = call(
        functools.partial(backward_kernel, cap),
        "backward",
        [half, half, ((1, places), F32)],
        (here, got_second, down, x, act, by_gate, by_up),
        scratch=(row_shape, ((places, 2 * hid), BF16)),
        scalars=1,
        flops=2**31,
        moved=12 * MB,
    )
    other = shifted(send, "core", 2, 1, 1)
    pair = ((2, block, 3 * hid), BF16)
    sums = call(pair_kernel, "pairs", [pair] * n_x, (keep, other), moved=8 * MB)
    order = [k for k in sorted(range(1, n_x), key=lambda k: -min(k, n_x - k))]
    terms = [shifted(sums[k], "x", n_x, 1, k) for k in order]
    single = ((block, 3 * hid), BF16)
    near, far = call(sum_kernel, "sums", [single] * 2, (sums[0], *terms), moved=3 * MB)
    far = shifted(far, "yh", 2, 1, 1)
    values = jnp.concatenate(spread(value, "yl", n_yl, 1), axis=0)
    values = jnp.concatenate(spread(values, "z", n_high, n_low), axis=0)
    values = spread(values, "z", n_low, 1)
    gate_up_grad, down_grad = call(
        functools.partial(finish_kernel, hid),
        "finish",
        [((block, 2 * hid), BF16), ((hid, block), BF16)],
        (near, far),
        moved=MB,
    )
    gate_grads = call(
        functools.partial(gate_grad_kernel, cap, (n_yl, n_high, n_low)),
        "gate_grad",
        [((1, tokens), F32)],
        (home, *values, row(routes_second), row(gates_second)),
        scalars=1,
        moved=MB // 8,
    )

    send_back = call(
        functools.partial(forward_kernel, cap),
        "forward",
        [chunk_shape],
        (got_first, gu, down),
        scratch=(row_shape,),
        after=tuple(terms),
        flops=2**31,
        moved=7 * MB,
    )
    got_back = exchange(send_back)
    mixed_first = call(
        functools.partial(combine_kernel, cap),
        "combine",
        [((tokens, model), BF16)],
        (got_back, mix),
        scratch=(row_shape,),
        flops=2**29,
        moved=2 * MB,
    )
    return (
        mixed_first,
        gate_grads.reshape(tokens, 1),
        gate_up_grad[None],
        down_grad[None],
    )


def solution(mesh):
    n_ep, n_dp = mesh.devices.shape
    lows = 4
    n_x = n_dp // 4
    fine = Mesh(mesh.devices.reshape(lows, n_ep // lows, 2, n_x, 2), ALL)
    tokens = P(ALL, None)
    return jax.shard_map(
        functools.partial(local, n_x),
        mesh=fine,
        in_specs=(
            tokens,
            tokens,
            tokens,
            P(EP, None, None),
            P(EP, None, None),
            P(EP, ("yh", "x", "core"), None, None),
            tokens,
            tokens,
            tokens,
        ),
        out_specs=(
            tokens,
            tokens,
            P(EP, ("yh", "x", "core"), None),
            P(EP, None, ("yh", "x", "core")),
        ),
        check_vma=False,
    )
```

```python
import functools

import jax
import jax.numpy as jnp
from jax import lax
from jax.experimental import pallas as pl
from jax.experimental.pallas import tpu as pltpu
from jax.sharding import Mesh, PartitionSpec as P

BF16 = jnp.bfloat16
F32 = jnp.float32
I32 = jnp.int32
EP = ("yl", "z")
ALL = ("yl", "z", "yh", "x", "core")
CHUNK = 8
EXTRA = 128


def iota(shape, dim):
    return lax.broadcasted_iota(I32, shape, dim)


def dot(a, b, ca=1, cb=0):
    return lax.dot_general(a, b, (((ca,), (cb,)), ((), ())), preferred_element_type=F32)


def slots_of(routes, experts):
    tokens = routes.shape[1]
    onehot = (iota((experts, tokens), 0) == routes).astype(F32)
    earlier = (iota((tokens, tokens), 0) < iota((tokens, tokens), 1)).astype(F32)
    before = dot(onehot.astype(BF16), earlier.astype(BF16))
    return onehot, jnp.sum(onehot * before, axis=0, keepdims=True).astype(I32)


def order_of(rows, cap, dim):
    j = iota((rows, rows), dim)
    per = rows * cap // CHUNK
    return j % CHUNK // cap * per + j // CHUNK * cap + j % cap


GROUP = 256


def from_chunks(chunks_ref, rows_ref, cap):
    width = chunks_ref.shape[1]
    pieces = CHUNK // cap
    per = GROUP // pieces
    order = (iota((GROUP, GROUP), 0) == order_of(GROUP, cap, 1)).astype(F32)
    order = order.astype(BF16)
    for g in range(chunks_ref.shape[0] // GROUP):
        part = dot(order, chunks_ref[g * GROUP : (g + 1) * GROUP, :]).astype(BF16)
        for q in range(pieces):
            rows_ref[g * per : (g + 1) * per, q * width : (q + 1) * width] = part[
                q * per : (q + 1) * per
            ]


def to_chunks(rows_ref, chunks_ref, cap):
    width = chunks_ref.shape[1]
    pieces = CHUNK // cap
    per = GROUP // pieces
    order = (iota((GROUP, GROUP), 1) == order_of(GROUP, cap, 0)).astype(F32)
    order = order.astype(BF16)
    for g in range(chunks_ref.shape[0] // GROUP):
        part = jnp.concatenate(
            [
                rows_ref[g * per : (g + 1) * per, q * width : (q + 1) * width]
                for q in range(pieces)
            ],
            axis=0,
        )
        chunks_ref[g * GROUP : (g + 1) * GROUP, :] = dot(order, part).astype(BF16)


def send_rows(experts, cap, routes, weights, tokens_ref, chunks_ref):
    tokens = routes.shape[1]
    width = chunks_ref.shape[1]
    _, slots = slots_of(routes, experts)
    base = routes * CHUNK + slots
    for g in range(chunks_ref.shape[0] // GROUP):
        row = iota((GROUP, tokens), 0) + g * GROUP
        total = None
        for q in range(CHUNK // cap):
            select = jnp.where(row == base + q * cap, weights, 0.0).astype(BF16)
            term = dot(select, tokens_ref[:, q * width : (q + 1) * width])
            total = term if total is None else total + term
        chunks_ref[g * GROUP : (g + 1) * GROUP, :] = total.astype(BF16)
    return slots


def dispatch_second_kernel(
    experts, cap, routes_ref, gates_ref, tokens_ref, chunks_ref
):
    send_rows(experts, cap, routes_ref[...], gates_ref[...].astype(F32), tokens_ref, chunks_ref)


def dispatch_first_kernel(
    experts,
    cap,
    routes_ref,
    gates_ref,
    other_routes_ref,
    tokens_ref,
    chunks_ref,
    mix_ref,
    pick_ref,
):
    routes = routes_ref[...]
    slots = send_rows(
        experts, cap, routes, jnp.ones(routes.shape, F32), tokens_ref, chunks_ref
    )
    place = iota((experts * cap, routes.shape[1]), 0)
    hit = place == routes * cap + slots
    mix_ref[...] = jnp.where(hit, gates_ref[...].astype(F32), 0.0).T.astype(BF16)
    routes = other_routes_ref[...]
    _, slots = slots_of(routes, experts)
    pick_ref[...] = (place == routes * cap + slots).astype(F32).T.astype(BF16)


def saved_kernel(x_ref, gu_ref, act_ref, gate_ref, up_ref):
    hid = act_ref.shape[1]
    both = dot(x_ref[...], gu_ref[...])
    gate, up = both[:, :hid], both[:, hid:]
    squash = jax.nn.sigmoid(gate)
    swish = gate * squash
    act_ref[...] = (swish * up).astype(BF16)
    gate_ref[...] = up * squash * (1.0 + gate * (1.0 - squash))
    up_ref[...] = swish


def backward_kernel(
    cap,
    at_ref,
    chunks_ref,
    down_ref,
    x_ref,
    act_ref,
    gate_ref,
    up_ref,
    keep_ref,
    send_ref,
    value_ref,
    rows_ref,
    both_ref,
):
    hid = act_ref.shape[1]
    block = keep_ref.shape[1]
    core, y, x = at_ref[0], at_ref[1], at_ref[2]
    from_chunks(chunks_ref, rows_ref, cap)
    scaled = dot(rows_ref[...], down_ref[...], 1, 1)
    value = jnp.sum(scaled * act_ref[...].astype(F32), axis=1, keepdims=True)
    lane = iota(value_ref.shape, 1)
    parts = jnp.zeros(value_ref.shape, F32)
    for k in range(3):
        part = value.astype(BF16).astype(F32)
        parts = jnp.where(lane == k, part, parts)
        value = value - part
    value_ref[...] = parts.astype(BF16)
    both_ref[:, :hid] = (scaled * gate_ref[...]).astype(BF16)
    both_ref[:, hid:] = (scaled * up_ref[...]).astype(BF16)
    n_x = keep_ref.shape[0] // 2
    for out_ref, other in ((send_ref, 1), (keep_ref, 0)):
        for n in range(2 * n_x):
            to = ((y + n % 2) % 2 * n_x + (x + n // 2) % n_x) * 2 + (core + other) % 2
            columns = pl.ds(pl.multiple_of(to * block, block), block)
            out_ref[n, :, : 2 * hid] = dot(x_ref[:, columns], both_ref[...], 0, 0).astype(BF16)
            out_ref[n, :, 2 * hid :] = dot(rows_ref[:, columns], act_ref[...], 0, 0).astype(BF16)


def forward_kernel(cap, chunks_ref, gu_ref, down_ref, value_ref, *refs):
    out_ref, in_rows_ref, out_rows_ref = refs[-3:]
    model, hid = down_ref.shape[1], down_ref.shape[0]
    from_chunks(chunks_ref, in_rows_ref, cap)
    both = dot(in_rows_ref[...], gu_ref[...])
    act = (jax.nn.silu(both[:, :hid]) * both[:, hid:]).astype(BF16)
    width = chunks_ref.shape[1]
    for q in range(model // width):
        at = q * (width + EXTRA)
        out_rows_ref[:, at : at + width] = dot(
            act, down_ref[:, q * width : (q + 1) * width]
        ).astype(BF16)
        out_rows_ref[:, at + width : at + width + EXTRA] = value_ref[...]
    to_chunks(out_rows_ref, out_ref, cap)


def combine_kernel(
    cap, chunks_ref, mix_ref, pick_ref, gates_ref, out_ref, grads_ref, rows_ref
):
    from_chunks(chunks_ref, rows_ref, cap)
    width = chunks_ref.shape[1] - EXTRA
    for q in range(CHUNK // cap):
        at = q * (width + EXTRA)
        out_ref[:, q * width : (q + 1) * width] = dot(
            mix_ref[...], rows_ref[:, at : at + width]
        ).astype(BF16)
    value = dot(pick_ref[...], rows_ref[:, width : width + EXTRA])
    value = jnp.sum(value.T, axis=0, keepdims=True)
    grads_ref[...] = value / gates_ref[...].astype(F32)


def pair_kernel(a_ref, b_ref, *out_refs):
    for k, out_ref in enumerate(out_refs):
        total = a_ref[2 * k : 2 * k + 2].astype(F32) + b_ref[2 * k : 2 * k + 2].astype(F32)
        out_ref[...] = total.astype(BF16)


def sum_kernel(*refs):
    *terms, near_ref, far_ref = refs
    for k, out_ref in ((1, far_ref), (0, near_ref)):
        total = terms[0][k].astype(F32)
        for term in terms[1:]:
            total = total + term[k].astype(F32)
        out_ref[...] = total.astype(BF16)


def finish_kernel(hid, a_ref, b_ref, gu_ref, down_ref):
    total = a_ref[...].astype(F32) + b_ref[...].astype(F32)
    gu_ref[...] = total[:, : 2 * hid].astype(BF16)
    down_ref[...] = total[:, 2 * hid :].T.astype(BF16)


VMEM = pl.BlockSpec(memory_space=pltpu.VMEM)
SMEM = pl.BlockSpec(memory_space=pltpu.SMEM)
ANY = pl.BlockSpec(memory_space=pl.ANY)


def call(kernel, name, outs, args, scratch=(), scalars=0, after=(), flops=0, moved=0):
    shapes = [jax.ShapeDtypeStruct(*o) for o in outs]
    result = pl.pallas_call(
        kernel,
        name=name,
        out_shape=shapes,
        in_specs=[SMEM] * scalars + [VMEM] * (len(args) - scalars) + [ANY] * len(after),
        out_specs=[VMEM] * len(outs),
        scratch_shapes=[pltpu.VMEM(*s) for s in scratch],
        compiler_params=pltpu.CompilerParams(vmem_limit_bytes=24 * 2**20),
        cost_estimate=pl.CostEstimate(flops=flops, bytes_accessed=moved, transcendentals=0),
    )(*args, *after)
    return result[0] if len(outs) == 1 else result


def local(
    n_x,
    tokens_first,
    routes_first,
    gates_first,
    gate_up_weight,
    down_weight,
    saved_inputs,
    upstream,
    routes_second,
    gates_second,
):
    experts = lax.axis_size("yl") * lax.axis_size("z")
    places, model = saved_inputs.shape[2:]
    cap = places // experts
    tokens = tokens_first.shape[0]
    width = model * cap // CHUNK
    gu, down, x = gate_up_weight[0], down_weight[0], saved_inputs[0, 0]
    hid = down.shape[0]
    block = model // (4 * n_x)
    MB = 2**20

    def row(a):
        return a.reshape(1, tokens)

    def exchange(chunks):
        wide = chunks.shape[1]
        chunks = chunks.reshape(experts, CHUNK, wide)
        moved = lax.all_to_all(chunks, EP, split_axis=0, concat_axis=0, tiled=True)
        return moved.reshape(experts * CHUNK, wide)

    def shifted(a, axis, k):
        size = lax.axis_size(axis)
        return lax.ppermute(a, axis, [(i, (i + k) % size) for i in range(size)])

    chunk_shape = ((experts * CHUNK, width), BF16)
    back_shape = ((experts * CHUNK, width + EXTRA), BF16)
    row_shape = ((places, model), BF16)
    back_rows = ((places, model + CHUNK // cap * EXTRA), BF16)
    extra_shape = ((places, EXTRA), BF16)
    pick_shape = ((tokens, places), BF16)
    here = jnp.stack(
        [lax.axis_index("core"), lax.axis_index("yh"), lax.axis_index("x")]
    ).astype(I32)

    send_second = call(
        functools.partial(dispatch_second_kernel, experts, cap),
        "dispatch_second",
        [chunk_shape],
        (row(routes_second), row(gates_second), upstream),
        flops=2**29,
        moved=2 * MB,
    )
    got_second = exchange(send_second)
    send_first, mix, pick = call(
        functools.partial(dispatch_first_kernel, experts, cap),
        "dispatch_first",
        [chunk_shape, pick_shape, pick_shape],
        (row(routes_first), row(gates_first), row(routes_second), tokens_first),
        flops=2**29,
        moved=2 * MB,
    )
    act, by_gate, by_up = call(
        saved_kernel,
        "saved",
        [((places, hid), BF16), ((places, hid), F32), ((places, hid), F32)],
        (x, gu),
        flops=2**30,
        moved=6 * MB,
    )
    got_first = exchange(send_first)

    half = ((2 * n_x, block, 3 * hid), BF16)
    keep, send, value = call(
        functools.partial(backward_kernel, cap),
        "backward",
        [half, half, extra_shape],
        (here, got_second, down, x, act, by_gate, by_up),
        scratch=(row_shape, ((places, 2 * hid), BF16)),
        scalars=1,
        flops=2**31,
        moved=12 * MB,
    )
    other = shifted(send, "core", 1)
    pair = ((2, block, 3 * hid), BF16)
    sums = call(pair_kernel, "pairs", [pair] * n_x, (keep, other), moved=8 * MB)
    order = sorted(range(1, n_x), key=lambda k: -min(k, n_x - k))
    terms = [shifted(sums[k], "x", k) for k in order]
    single = ((block, 3 * hid), BF16)
    near, far = call(sum_kernel, "sums", [single] * 2, (sums[0], *terms), moved=3 * MB)
    far = shifted(far, "yh", 1)
    gate_up_grad, down_grad = call(
        functools.partial(finish_kernel, hid),
        "finish",
        [((block, 2 * hid), BF16), ((hid, block), BF16)],
        (near, far),
        moved=MB,
    )
    send_back = call(
        functools.partial(forward_kernel, cap),
        "forward",
        [back_shape],
        (got_first, gu, down, value),
        scratch=(row_shape, back_rows),
        after=tuple(terms),
        flops=2**31,
        moved=7 * MB,
    )
    got_back = exchange(send_back)
    mixed_first, gate_grads = call(
        functools.partial(combine_kernel, cap),
        "combine",
        [((tokens, model), BF16), ((1, tokens), F32)],
        (got_back, mix, pick, row(gates_second)),
        scratch=(back_rows,),
        flops=2**29,
        moved=2 * MB,
    )
    return (
        mixed_first,
        gate_grads.reshape(tokens, 1),
        gate_up_grad[None],
        down_grad[None],
    )


def solution(mesh):
    n_ep, n_dp = mesh.devices.shape
    lows = 4
    n_x = n_dp // 4
    fine = Mesh(mesh.devices.reshape(lows, n_ep // lows, 2, n_x, 2), ALL)
    tokens = P(ALL, None)
    return jax.shard_map(
        functools.partial(local, n_x),
        mesh=fine,
        in_specs=(
            tokens,
            tokens,
            tokens,
            P(EP, None, None),
            P(EP, None, None),
            P(EP, ("yh", "x", "core"), None, None),
            tokens,
            tokens,
            tokens,
        ),
        out_specs=(
            tokens,
            tokens,
            P(EP, ("yh", "x", "core"), None),
            P(EP, None, ("yh", "x", "core")),
        ),
        check_vma=False,
    )
```

```python
import functools

import jax
import jax.numpy as jnp
from jax import lax
from jax.experimental import pallas as pl
from jax.experimental.pallas import tpu as pltpu
from jax.sharding import Mesh, PartitionSpec as P

BF16 = jnp.bfloat16
F32 = jnp.float32
I32 = jnp.int32
EP = ("yl", "z")
ALL = ("yl", "z", "yh", "x", "core")
CHUNK = 8
EXTRA = 128


def iota(shape, dim):
    return lax.broadcasted_iota(I32, shape, dim)


def dot(a, b, ca=1, cb=0):
    return lax.dot_general(a, b, (((ca,), (cb,)), ((), ())), preferred_element_type=F32)


def start_copy(source, target, semaphore):
    copy = pltpu.make_async_copy(source, target, semaphore)
    copy.start()
    return copy


def group(ref, g):
    return ref.at[pl.ds(g * GROUP, GROUP)]


def slots_of(routes, experts):
    tokens = routes.shape[1]
    onehot = (iota((experts, tokens), 0) == routes).astype(F32)
    earlier = (iota((tokens, tokens), 0) < iota((tokens, tokens), 1)).astype(F32)
    before = dot(onehot.astype(BF16), earlier.astype(BF16))
    return onehot, jnp.sum(onehot * before, axis=0, keepdims=True).astype(I32)


def order_of(rows, cap, dim):
    j = iota((rows, rows), dim)
    per = rows * cap // CHUNK
    return j % CHUNK // cap * per + j // CHUNK * cap + j % cap


GROUP = 256


def from_chunks(chunks_ref, rows_ref, cap, arrivals=None):
    width = chunks_ref.shape[1]
    pieces = CHUNK // cap
    per = GROUP // pieces
    order = (iota((GROUP, GROUP), 0) == order_of(GROUP, cap, 1)).astype(F32)
    order = order.astype(BF16)
    for g in range(chunks_ref.shape[0] // GROUP):
        if arrivals:
            arrivals[g].wait()
        part = dot(order, chunks_ref[g * GROUP : (g + 1) * GROUP, :]).astype(BF16)
        for q in range(pieces):
            rows_ref[g * per : (g + 1) * per, q * width : (q + 1) * width] = part[
                q * per : (q + 1) * per
            ]


def to_chunks(rows_ref, chunks_ref, out_ref, semaphores, cap):
    width = chunks_ref.shape[1]
    pieces = CHUNK // cap
    per = GROUP // pieces
    copies = []
    order = (iota((GROUP, GROUP), 1) == order_of(GROUP, cap, 0)).astype(F32)
    order = order.astype(BF16)
    for g in range(chunks_ref.shape[0] // GROUP):
        part = jnp.concatenate(
            [
                rows_ref[g * per : (g + 1) * per, q * width : (q + 1) * width]
                for q in range(pieces)
            ],
            axis=0,
        )
        chunks_ref[g * GROUP : (g + 1) * GROUP, :] = dot(order, part).astype(BF16)
        copies.append(start_copy(group(chunks_ref, g), group(out_ref, g), semaphores.at[g]))
    for copy in copies:
        copy.wait()


def send_rows(
    experts, cap, routes, weights, tokens_ref, chunks_ref, out_ref, semaphores, arrival
):
    tokens = routes.shape[1]
    width = chunks_ref.shape[1]
    _, slots = slots_of(routes, experts)
    base = routes * CHUNK + slots
    copies = []
    arrival.wait()
    for g in range(chunks_ref.shape[0] // GROUP):
        row = iota((GROUP, tokens), 0) + g * GROUP
        total = None
        for q in range(CHUNK // cap):
            select = jnp.where(row == base + q * cap, weights, 0.0).astype(BF16)
            term = dot(select, tokens_ref[:, q * width : (q + 1) * width])
            total = term if total is None else total + term
        chunks_ref[g * GROUP : (g + 1) * GROUP, :] = total.astype(BF16)
        copies.append(start_copy(group(chunks_ref, g), group(out_ref, g), semaphores.at[g]))
    return slots, copies


def dispatch_second_kernel(
    experts,
    cap,
    routes_hbm,
    gates_hbm,
    tokens_hbm,
    out_ref,
    routes_ref,
    gates_ref,
    tokens_ref,
    chunks_ref,
    in_semaphores,
    out_semaphores,
):
    pairs = ((routes_hbm, routes_ref), (gates_hbm, gates_ref), (tokens_hbm, tokens_ref))
    first, second, third = [
        start_copy(a, b, in_semaphores.at[k]) for k, (a, b) in enumerate(pairs)
    ]
    first.wait()
    second.wait()
    _, copies = send_rows(
        experts,
        cap,
        routes_ref[...],
        gates_ref[...].astype(F32),
        tokens_ref,
        chunks_ref,
        out_ref,
        out_semaphores,
        third,
    )
    for copy in copies:
        copy.wait()


def dispatch_first_kernel(
    experts,
    cap,
    routes_ref,
    gates_ref,
    other_routes_ref,
    tokens_hbm,
    out_ref,
    mix_ref,
    pick_ref,
    tokens_ref,
    chunks_ref,
    in_semaphores,
    out_semaphores,
):
    arrival = start_copy(tokens_hbm, tokens_ref, in_semaphores.at[0])
    routes = routes_ref[...]
    slots, copies = send_rows(
        experts,
        cap,
        routes,
        jnp.ones(routes.shape, F32),
        tokens_ref,
        chunks_ref,
        out_ref,
        out_semaphores,
        arrival,
    )
    place = iota((experts * cap, routes.shape[1]), 0)
    hit = place == routes * cap + slots
    mix_ref[...] = jnp.where(hit, gates_ref[...].astype(F32), 0.0).T.astype(BF16)
    routes = other_routes_ref[...]
    _, slots = slots_of(routes, experts)
    pick_ref[...] = (place == routes * cap + slots).astype(F32).T.astype(BF16)
    for copy in copies:
        copy.wait()


def saved_kernel(x_ref, gu_ref, act_ref, gate_ref, up_ref):
    hid = act_ref.shape[1]
    both = dot(x_ref[...], gu_ref[...])
    gate, up = both[:, :hid], both[:, hid:]
    squash = jax.nn.sigmoid(gate)
    swish = gate * squash
    act_ref[...] = (swish * up).astype(BF16)
    gate_ref[...] = up * squash * (1.0 + gate * (1.0 - squash))
    up_ref[...] = swish


def backward_kernel(
    cap,
    at_ref,
    chunks_ref,
    down_ref,
    x_ref,
    act_ref,
    gate_ref,
    up_ref,
    keep_ref,
    send_ref,
    value_ref,
    rows_ref,
    both_ref,
):
    hid = act_ref.shape[1]
    block = keep_ref.shape[1]
    core, y, x = at_ref[0], at_ref[1], at_ref[2]
    from_chunks(chunks_ref, rows_ref, cap)
    scaled = dot(rows_ref[...], down_ref[...], 1, 1)
    value = jnp.sum(scaled * act_ref[...].astype(F32), axis=1, keepdims=True)
    lane = iota(value_ref.shape, 1)
    parts = jnp.zeros(value_ref.shape, F32)
    for k in range(3):
        part = value.astype(BF16).astype(F32)
        parts = jnp.where(lane == k, part, parts)
        value = value - part
    value_ref[...] = parts.astype(BF16)
    both_ref[:, :hid] = (scaled * gate_ref[...]).astype(BF16)
    both_ref[:, hid:] = (scaled * up_ref[...]).astype(BF16)
    n_x = keep_ref.shape[0] // 2
    for out_ref, other in ((send_ref, 1), (keep_ref, 0)):
        for n in range(2 * n_x):
            to = ((y + n % 2) % 2 * n_x + (x + n // 2) % n_x) * 2 + (core + other) % 2
            columns = pl.ds(pl.multiple_of(to * block, block), block)
            out_ref[n, :, : 2 * hid] = dot(x_ref[:, columns], both_ref[...], 0, 0).astype(BF16)
            out_ref[n, :, 2 * hid :] = dot(rows_ref[:, columns], act_ref[...], 0, 0).astype(BF16)


def forward_kernel(cap, chunks_hbm, gu_ref, down_hbm, value_ref, *refs):
    out_ref, chunks_ref, down_ref, back_ref, in_rows_ref, out_rows_ref = refs[-8:-2]
    in_semaphores, out_semaphores = refs[-2:]
    groups = chunks_ref.shape[0] // GROUP
    arrivals = [
        start_copy(group(chunks_hbm, g), group(chunks_ref, g), in_semaphores.at[g])
        for g in range(groups)
    ]
    down_arrival = start_copy(down_hbm, down_ref, in_semaphores.at[groups])
    model, hid = down_ref.shape[1], down_ref.shape[0]
    from_chunks(chunks_ref, in_rows_ref, cap, arrivals)
    both = dot(in_rows_ref[...], gu_ref[...])
    act = (jax.nn.silu(both[:, :hid]) * both[:, hid:]).astype(BF16)
    width = chunks_ref.shape[1]
    down_arrival.wait()
    for q in range(model // width):
        at = q * (width + EXTRA)
        out_rows_ref[:, at : at + width] = dot(
            act, down_ref[:, q * width : (q + 1) * width]
        ).astype(BF16)
        out_rows_ref[:, at + width : at + width + EXTRA] = value_ref[...]
    to_chunks(out_rows_ref, back_ref, out_ref, out_semaphores, cap)


def combine_kernel(
    cap, chunks_ref, mix_ref, pick_ref, gates_ref, out_ref, grads_ref, rows_ref
):
    from_chunks(chunks_ref, rows_ref, cap)
    width = chunks_ref.shape[1] - EXTRA
    for q in range(CHUNK // cap):
        at = q * (width + EXTRA)
        out_ref[:, q * width : (q + 1) * width] = dot(
            mix_ref[...], rows_ref[:, at : at + width]
        ).astype(BF16)
    value = dot(pick_ref[...], rows_ref[:, width : width + EXTRA])
    value = jnp.sum(value.T, axis=0, keepdims=True)
    grads_ref[...] = value / gates_ref[...].astype(F32)


def pair_kernel(a_ref, b_ref, *out_refs):
    for k, out_ref in enumerate(out_refs):
        total = a_ref[2 * k : 2 * k + 2].astype(F32) + b_ref[2 * k : 2 * k + 2].astype(F32)
        out_ref[...] = total.astype(BF16)


def sum_kernel(*refs):
    *terms, near_ref, far_ref = refs
    for k, out_ref in ((1, far_ref), (0, near_ref)):
        total = terms[0][k].astype(F32)
        for term in terms[1:]:
            total = total + term[k].astype(F32)
        out_ref[...] = total.astype(BF16)


def finish_kernel(hid, a_ref, b_ref, gu_ref, down_ref):
    total = a_ref[...].astype(F32) + b_ref[...].astype(F32)
    gu_ref[...] = total[:, : 2 * hid].astype(BF16)
    down_ref[...] = total[:, 2 * hid :].T.astype(BF16)


VMEM = pl.BlockSpec(memory_space=pltpu.VMEM)
SMEM = pl.BlockSpec(memory_space=pltpu.SMEM)
ANY = pl.BlockSpec(memory_space=pl.ANY)
HBM = pl.BlockSpec(memory_space=pltpu.HBM)


def call(
    kernel,
    name,
    outs,
    args,
    scratch=(),
    scalars=0,
    after=(),
    hbm_in=(),
    hbm_out=(),
    semaphores=(),
    limit=16,
    flops=0,
    moved=0,
):
    shapes = [
        pltpu.HBM(*o) if k in hbm_out else jax.ShapeDtypeStruct(*o) for k, o in enumerate(outs)
    ]
    args = [
        pltpu.with_memory_space_constraint(a, pltpu.HBM) if k in hbm_in else a
        for k, a in enumerate(args)
    ]
    spaces = [SMEM if k < scalars else HBM if k in hbm_in else VMEM for k in range(len(args))]
    result = pl.pallas_call(
        kernel,
        name=name,
        out_shape=shapes,
        in_specs=spaces + [ANY] * len(after),
        out_specs=[HBM if k in hbm_out else VMEM for k in range(len(outs))],
        scratch_shapes=[pltpu.VMEM(*s) for s in scratch]
        + [pltpu.SemaphoreType.DMA((n,)) for n in semaphores],
        compiler_params=pltpu.CompilerParams(vmem_limit_bytes=limit * 2**20),
        cost_estimate=pl.CostEstimate(flops=flops, bytes_accessed=moved, transcendentals=0),
    )(*args, *after)
    return result[0] if len(outs) == 1 else result


def local(
    n_x,
    tokens_first,
    routes_first,
    gates_first,
    gate_up_weight,
    down_weight,
    saved_inputs,
    upstream,
    routes_second,
    gates_second,
):
    experts = lax.axis_size("yl") * lax.axis_size("z")
    places, model = saved_inputs.shape[2:]
    cap = places // experts
    tokens = tokens_first.shape[0]
    width = model * cap // CHUNK
    gu, down, x = gate_up_weight[0], down_weight[0], saved_inputs[0, 0]
    hid = down.shape[0]
    block = model // (4 * n_x)
    MB = 2**20
    groups = experts * CHUNK // GROUP

    def row(a):
        return a.reshape(1, tokens)

    def exchange(chunks):
        wide = chunks.shape[1]
        chunks = chunks.reshape(experts, CHUNK, wide)
        moved = lax.all_to_all(chunks, EP, split_axis=0, concat_axis=0, tiled=True)
        return moved.reshape(experts * CHUNK, wide)

    def shifted(a, axis, k):
        size = lax.axis_size(axis)
        return lax.ppermute(a, axis, [(i, (i + k) % size) for i in range(size)])

    chunk_shape = ((experts * CHUNK, width), BF16)
    back_shape = ((experts * CHUNK, width + EXTRA), BF16)
    row_shape = ((places, model), BF16)
    back_rows = ((places, model + CHUNK // cap * EXTRA), BF16)
    extra_shape = ((places, EXTRA), BF16)
    pick_shape = ((tokens, places), BF16)
    here = jnp.stack(
        [lax.axis_index("core"), lax.axis_index("yh"), lax.axis_index("x")]
    ).astype(I32)

    send_second = call(
        functools.partial(dispatch_second_kernel, experts, cap),
        "dispatch_second",
        [chunk_shape],
        (row(routes_second), row(gates_second), upstream),
        scratch=(
            ((1, tokens), I32),
            ((1, tokens), BF16),
            ((tokens, model), BF16),
            chunk_shape,
        ),
        hbm_in=(0, 1, 2),
        hbm_out=(0,),
        semaphores=(3, groups),
        flops=2**29,
        moved=2 * MB,
    )
    got_second = exchange(send_second)
    send_first, mix, pick = call(
        functools.partial(dispatch_first_kernel, experts, cap),
        "dispatch_first",
        [chunk_shape, pick_shape, pick_shape],
        (row(routes_first), row(gates_first), row(routes_second), tokens_first),
        scratch=(((tokens, model), BF16), chunk_shape),
        hbm_in=(3,),
        hbm_out=(0,),
        semaphores=(1, groups),
        flops=2**29,
        moved=2 * MB,
    )
    act, by_gate, by_up = call(
        saved_kernel,
        "saved",
        [((places, hid), BF16), ((places, hid), F32), ((places, hid), F32)],
        (x, gu),
        flops=2**30,
        moved=6 * MB,
    )
    got_first = exchange(send_first)

    half = ((2 * n_x, block, 3 * hid), BF16)
    keep, send, value = call(
        functools.partial(backward_kernel, cap),
        "backward",
        [half, half, extra_shape],
        (here, got_second, down, x, act, by_gate, by_up),
        scratch=(row_shape, ((places, 2 * hid), BF16)),
        scalars=1,
        flops=2**31,
        moved=12 * MB,
    )
    other = shifted(send, "core", 1)
    pair = ((2, block, 3 * hid), BF16)
    sums = call(pair_kernel, "pairs", [pair] * n_x, (keep, other), moved=8 * MB)
    order = sorted(range(1, n_x), key=lambda k: -min(k, n_x - k))
    terms = [shifted(sums[k], "x", k) for k in order]
    single = ((block, 3 * hid), BF16)
    near, far = call(sum_kernel, "sums", [single] * 2, (sums[0], *terms), moved=3 * MB)
    far = shifted(far, "yh", 1)
    gate_up_grad, down_grad = call(
        functools.partial(finish_kernel, hid),
        "finish",
        [((block, 2 * hid), BF16), ((hid, block), BF16)],
        (near, far),
        moved=MB,
    )
    send_back = call(
        functools.partial(forward_kernel, cap),
        "forward",
        [back_shape],
        (got_first, gu, down, value),
        scratch=(chunk_shape, ((hid, model), BF16), back_shape, row_shape, back_rows),
        after=tuple(terms),
        hbm_in=(0, 2),
        hbm_out=(0,),
        semaphores=(groups + 1, groups),
        flops=2**31,
        moved=7 * MB,
    )
    got_back = exchange(send_back)
    mixed_first, gate_grads = call(
        functools.partial(combine_kernel, cap),
        "combine",
        [((tokens, model), BF16), ((1, tokens), F32)],
        (got_back, mix, pick, row(gates_second)),
        scratch=(back_rows,),
        flops=2**29,
        moved=2 * MB,
    )
    return (
        mixed_first,
        gate_grads.reshape(tokens, 1),
        gate_up_grad[None],
        down_grad[None],
    )


def solution(mesh):
    n_ep, n_dp = mesh.devices.shape
    lows = 4
    n_x = n_dp // 4
    fine = Mesh(mesh.devices.reshape(lows, n_ep // lows, 2, n_x, 2), ALL)
    tokens = P(ALL, None)
    return jax.shard_map(
        functools.partial(local, n_x),
        mesh=fine,
        in_specs=(
            tokens,
            tokens,
            tokens,
            P(EP, None, None),
            P(EP, None, None),
            P(EP, ("yh", "x", "core"), None, None),
            tokens,
            tokens,
            tokens,
        ),
        out_specs=(
            tokens,
            tokens,
            P(EP, ("yh", "x", "core"), None),
            P(EP, None, ("yh", "x", "core")),
        ),
        check_vma=False,
    )
```

```python
import functools

import jax
import jax.numpy as jnp
from jax import lax
from jax.experimental import pallas as pl
from jax.experimental.pallas import tpu as pltpu
from jax.sharding import Mesh, PartitionSpec as P

BF16 = jnp.bfloat16
F32 = jnp.float32
I32 = jnp.int32
EP = ("yl", "z")
ALL = ("yl", "z", "yh", "x", "core")
CHUNK = 8
EARLY = 3


def iota(shape, dim):
    return lax.broadcasted_iota(I32, shape, dim)


def dot(a, b, ca=1, cb=0):
    return lax.dot_general(a, b, (((ca,), (cb,)), ((), ())), preferred_element_type=F32)


def start_copy(source, target, semaphore):
    copy = pltpu.make_async_copy(source, target, semaphore)
    copy.start()
    return copy


def group(ref, g):
    return ref.at[pl.ds(g * GROUP, GROUP)]


def slots_of(routes, experts):
    tokens = routes.shape[1]
    onehot = (iota((experts, tokens), 0) == routes).astype(F32)
    earlier = (iota((tokens, tokens), 0) < iota((tokens, tokens), 1)).astype(F32)
    before = dot(onehot.astype(BF16), earlier.astype(BF16))
    return onehot, jnp.sum(onehot * before, axis=0, keepdims=True).astype(I32)


def order_of(rows, cap, dim):
    j = iota((rows, rows), dim)
    per = rows * cap // CHUNK
    return j % CHUNK // cap * per + j // CHUNK * cap + j % cap


GROUP = 256


def from_chunks(chunks_ref, rows_ref, cap, arrivals=None):
    width = chunks_ref.shape[1]
    pieces = CHUNK // cap
    per = GROUP // pieces
    order = (iota((GROUP, GROUP), 0) == order_of(GROUP, cap, 1)).astype(F32)
    order = order.astype(BF16)
    for g in range(chunks_ref.shape[0] // GROUP):
        if arrivals:
            arrivals[g].wait()
        part = dot(order, chunks_ref[g * GROUP : (g + 1) * GROUP, :]).astype(BF16)
        for q in range(pieces):
            rows_ref[g * per : (g + 1) * per, q * width : (q + 1) * width] = part[
                q * per : (q + 1) * per
            ]


def to_chunks(rows_ref, chunks_ref, out_ref, semaphores, cap):
    width = chunks_ref.shape[1]
    pieces = CHUNK // cap
    per = GROUP // pieces
    copies = []
    order = (iota((GROUP, GROUP), 1) == order_of(GROUP, cap, 0)).astype(F32)
    order = order.astype(BF16)
    for g in range(chunks_ref.shape[0] // GROUP):
        part = jnp.concatenate(
            [
                rows_ref[g * per : (g + 1) * per, q * width : (q + 1) * width]
                for q in range(pieces)
            ],
            axis=0,
        )
        chunks_ref[g * GROUP : (g + 1) * GROUP, :] = dot(order, part).astype(BF16)
        copies.append(start_copy(group(chunks_ref, g), group(out_ref, g), semaphores.at[g]))
    for copy in copies:
        copy.wait()


def send_rows(
    experts, cap, routes, weights, tokens_ref, chunks_ref, out_ref, semaphores, arrival
):
    tokens = routes.shape[1]
    width = chunks_ref.shape[1]
    _, slots = slots_of(routes, experts)
    base = routes * CHUNK + slots
    copies = []
    arrival.wait()
    for g in range(chunks_ref.shape[0] // GROUP):
        row = iota((GROUP, tokens), 0) + g * GROUP
        total = None
        for q in range(CHUNK // cap):
            select = jnp.where(row == base + q * cap, weights, 0.0).astype(BF16)
            term = dot(select, tokens_ref[:, q * width : (q + 1) * width])
            total = term if total is None else total + term
        chunks_ref[g * GROUP : (g + 1) * GROUP, :] = total.astype(BF16)
        copies.append(start_copy(group(chunks_ref, g), group(out_ref, g), semaphores.at[g]))
    return slots, copies


def dispatch_second_kernel(
    experts,
    cap,
    routes_hbm,
    gates_hbm,
    tokens_hbm,
    out_ref,
    routes_ref,
    gates_ref,
    tokens_ref,
    chunks_ref,
    in_semaphores,
    out_semaphores,
):
    pairs = ((routes_hbm, routes_ref), (gates_hbm, gates_ref), (tokens_hbm, tokens_ref))
    first, second, third = [
        start_copy(a, b, in_semaphores.at[k]) for k, (a, b) in enumerate(pairs)
    ]
    first.wait()
    second.wait()
    _, copies = send_rows(
        experts,
        cap,
        routes_ref[...],
        gates_ref[...].astype(F32),
        tokens_ref,
        chunks_ref,
        out_ref,
        out_semaphores,
        third,
    )
    for copy in copies:
        copy.wait()


def dispatch_first_kernel(
    experts,
    cap,
    routes_ref,
    gates_ref,
    tokens_hbm,
    *refs,
):
    out_ref, mix_ref, tokens_ref, chunks_ref, in_semaphores, out_semaphores = refs[-6:]
    arrival = start_copy(tokens_hbm, tokens_ref, in_semaphores.at[0])
    routes = routes_ref[...]
    slots, copies = send_rows(
        experts,
        cap,
        routes,
        jnp.ones(routes.shape, F32),
        tokens_ref,
        chunks_ref,
        out_ref,
        out_semaphores,
        arrival,
    )
    place = iota((experts * cap, routes.shape[1]), 0)
    hit = place == routes * cap + slots
    mix_ref[...] = jnp.where(hit, gates_ref[...].astype(F32), 0.0).T.astype(BF16)
    for copy in copies:
        copy.wait()


def saved_kernel(x_ref, gu_ref, act_ref, gate_ref, up_ref):
    hid = act_ref.shape[1]
    both = dot(x_ref[...], gu_ref[...])
    gate, up = both[:, :hid], both[:, hid:]
    squash = jax.nn.sigmoid(gate)
    swish = gate * squash
    act_ref[...] = (swish * up).astype(BF16)
    gate_ref[...] = up * squash * (1.0 + gate * (1.0 - squash))
    up_ref[...] = swish


def backward_kernel(
    cap,
    at_ref,
    chunks_ref,
    down_ref,
    x_ref,
    act_ref,
    gate_ref,
    up_ref,
    keep_ref,
    send_ref,
    value_ref,
    rows_ref,
    both_ref,
):
    hid = act_ref.shape[1]
    block = keep_ref.shape[1]
    core, y, x = at_ref[0], at_ref[1], at_ref[2]
    from_chunks(chunks_ref, rows_ref, cap)
    scaled = dot(rows_ref[...], down_ref[...], 1, 1)
    product = scaled * act_ref[...].astype(F32)
    folded = product[:, :128]
    for k in range(1, hid // 128):
        folded = folded + product[:, k * 128 : (k + 1) * 128]
    value_ref[...] = jnp.sum(folded.T, axis=0, keepdims=True)
    both_ref[:, :hid] = (scaled * gate_ref[...]).astype(BF16)
    both_ref[:, hid:] = (scaled * up_ref[...]).astype(BF16)
    n_x = keep_ref.shape[0] // 2
    for out_ref, other in ((send_ref, 1), (keep_ref, 0)):
        for n in range(2 * n_x):
            to = ((y + n % 2) % 2 * n_x + (x + n // 2) % n_x) * 2 + (core + other) % 2
            columns = pl.ds(pl.multiple_of(to * block, block), block)
            out_ref[n, :, : 2 * hid] = dot(x_ref[:, columns], both_ref[...], 0, 0).astype(BF16)
            out_ref[n, :, 2 * hid :] = dot(rows_ref[:, columns], act_ref[...], 0, 0).astype(BF16)


def forward_kernel(cap, chunks_hbm, gu_ref, down_hbm, *refs):
    out_ref, chunks_ref, down_ref, back_ref, in_rows_ref, out_rows_ref = refs[-8:-2]
    in_semaphores, out_semaphores = refs[-2:]
    groups = chunks_ref.shape[0] // GROUP
    arrivals = [
        start_copy(group(chunks_hbm, g), group(chunks_ref, g), in_semaphores.at[g])
        for g in range(groups)
    ]
    down_arrival = start_copy(down_hbm, down_ref, in_semaphores.at[groups])
    hid = down_ref.shape[0]
    from_chunks(chunks_ref, in_rows_ref, cap, arrivals)
    both = dot(in_rows_ref[...], gu_ref[...])
    act = (jax.nn.silu(both[:, :hid]) * both[:, hid:]).astype(BF16)
    down_arrival.wait()
    out_rows_ref[...] = dot(act, down_ref[...]).astype(BF16)
    to_chunks(out_rows_ref, back_ref, out_ref, out_semaphores, cap)


def combine_kernel(cap, chunks_ref, mix_ref, out_ref, rows_ref):
    from_chunks(chunks_ref, rows_ref, cap)
    out_ref[...] = dot(mix_ref[...], rows_ref[...]).astype(BF16)


def gate_grad_kernel(cap, n_z, bits, at_ref, a_ref, b_ref, routes_ref, gates_ref, out_ref):
    values = jnp.concatenate([a_ref[...], b_ref[...]], axis=0)
    experts, places = values.shape
    routes = routes_ref[...]
    _, slots = slots_of(routes, experts)
    home = at_ref[0] * n_z + at_ref[1]
    apart = jnp.bitwise_xor(routes, home)
    source = jnp.zeros_like(routes)
    for r, bit in enumerate(bits):
        source = source + jnp.bitwise_and(jnp.right_shift(apart, bit), 1) * 2**r
    hit = (iota((experts, routes.shape[1]), 0) == source).astype(F32)
    lane = iota((experts, places), 1)
    total = jnp.zeros(out_ref.shape, F32)
    for c in range(cap):
        mine = jnp.sum(jnp.where(lane == home * cap + c, values, 0.0), axis=1, keepdims=True)
        here = jnp.sum(hit * mine, axis=0, keepdims=True)
        total = total + jnp.where(slots == c, here, 0.0)
    out_ref[...] = total / gates_ref[...].astype(F32)


def pair_kernel(a_ref, b_ref, *out_refs):
    for k, out_ref in enumerate(out_refs):
        total = a_ref[2 * k : 2 * k + 2].astype(F32) + b_ref[2 * k : 2 * k + 2].astype(F32)
        out_ref[...] = total.astype(BF16)


def sum_kernel(*refs):
    *terms, near_ref, far_ref = refs
    for k, out_ref in ((1, far_ref), (0, near_ref)):
        total = terms[0][k].astype(F32)
        for term in terms[1:]:
            total = total + term[k].astype(F32)
        out_ref[...] = total.astype(BF16)


def finish_kernel(hid, a_ref, b_ref, gu_ref, down_ref):
    total = a_ref[...].astype(F32) + b_ref[...].astype(F32)
    gu_ref[...] = total[:, : 2 * hid].astype(BF16)
    down_ref[...] = total[:, 2 * hid :].T.astype(BF16)


VMEM = pl.BlockSpec(memory_space=pltpu.VMEM)
SMEM = pl.BlockSpec(memory_space=pltpu.SMEM)
ANY = pl.BlockSpec(memory_space=pl.ANY)
HBM = pl.BlockSpec(memory_space=pltpu.HBM)


def call(
    kernel,
    name,
    outs,
    args,
    scratch=(),
    scalars=0,
    after=(),
    hbm_in=(),
    hbm_out=(),
    semaphores=(),
    limit=16,
    flops=0,
    moved=0,
):
    shapes = [
        pltpu.HBM(*o) if k in hbm_out else jax.ShapeDtypeStruct(*o) for k, o in enumerate(outs)
    ]
    args = [
        pltpu.with_memory_space_constraint(a, pltpu.HBM) if k in hbm_in else a
        for k, a in enumerate(args)
    ]
    spaces = [SMEM if k < scalars else HBM if k in hbm_in else VMEM for k in range(len(args))]
    result = pl.pallas_call(
        kernel,
        name=name,
        out_shape=shapes,
        in_specs=spaces + [ANY] * len(after),
        out_specs=[HBM if k in hbm_out else VMEM for k in range(len(outs))],
        scratch_shapes=[pltpu.VMEM(*s) for s in scratch]
        + [pltpu.SemaphoreType.DMA((n,)) for n in semaphores],
        compiler_params=pltpu.CompilerParams(vmem_limit_bytes=limit * 2**20),
        cost_estimate=pl.CostEstimate(flops=flops, bytes_accessed=moved, transcendentals=0),
    )(*args, *after)
    return result[0] if len(outs) == 1 else result


def local(
    n_x,
    tokens_first,
    routes_first,
    gates_first,
    gate_up_weight,
    down_weight,
    saved_inputs,
    upstream,
    routes_second,
    gates_second,
):
    experts = lax.axis_size("yl") * lax.axis_size("z")
    places, model = saved_inputs.shape[2:]
    cap = places // experts
    tokens = tokens_first.shape[0]
    width = model * cap // CHUNK
    gu, down, x = gate_up_weight[0], down_weight[0], saved_inputs[0, 0]
    hid = down.shape[0]
    block = model // (4 * n_x)
    MB = 2**20
    groups = experts * CHUNK // GROUP

    def row(a):
        return a.reshape(1, tokens)

    def exchange(chunks):
        wide = chunks.shape[1]
        chunks = chunks.reshape(experts, CHUNK, wide)
        moved = lax.all_to_all(chunks, EP, split_axis=0, concat_axis=0, tiled=True)
        return moved.reshape(experts * CHUNK, wide)

    def shifted(a, axis, k):
        size = lax.axis_size(axis)
        return lax.ppermute(a, axis, [(i, (i + k) % size) for i in range(size)])

    chunk_shape = ((experts * CHUNK, width), BF16)
    row_shape = ((places, model), BF16)
    here = jnp.stack(
        [lax.axis_index("core"), lax.axis_index("yh"), lax.axis_index("x")]
    ).astype(I32)

    send_second = call(
        functools.partial(dispatch_second_kernel, experts, cap),
        "dispatch_second",
        [chunk_shape],
        (row(routes_second), row(gates_second), upstream),
        scratch=(
            ((1, tokens), I32),
            ((1, tokens), BF16),
            ((tokens, model), BF16),
            chunk_shape,
        ),
        hbm_in=(0, 1, 2),
        hbm_out=(0,),
        semaphores=(3, groups),
        flops=2**29,
        moved=2 * MB,
    )
    got_second = exchange(send_second)
    act, by_gate, by_up = call(
        saved_kernel,
        "saved",
        [((places, hid), BF16), ((places, hid), F32), ((places, hid), F32)],
        (x, gu),
        flops=2**30,
        moved=6 * MB,
    )
    send_first, mix = call(
        functools.partial(dispatch_first_kernel, experts, cap),
        "dispatch_first",
        [chunk_shape, ((tokens, places), BF16)],
        (row(routes_first), row(gates_first), tokens_first),
        scratch=(((tokens, model), BF16), chunk_shape),
        after=(by_up,),
        hbm_in=(2,),
        hbm_out=(0,),
        semaphores=(1, groups),
        flops=2**29,
        moved=2 * MB,
    )
    got_first = exchange(send_first)

    half = ((2 * n_x, block, 3 * hid), BF16)
    keep, send, value = call(
        functools.partial(backward_kernel, cap),
        "backward",
        [half, half, ((1, places), F32)],
        (here, got_second, down, x, act, by_gate, by_up),
        scratch=(row_shape, ((places, 2 * hid), BF16)),
        scalars=1,
        flops=2**31,
        moved=12 * MB,
    )
    other = shifted(send, "core", 1)
    pair = ((2, block, 3 * hid), BF16)
    sums = call(pair_kernel, "pairs", [pair] * n_x, (keep, other), moved=8 * MB)
    order = sorted(range(1, n_x), key=lambda k: -min(k, n_x - k))
    terms = [shifted(sums[k], "x", k) for k in order]
    single = ((block, 3 * hid), BF16)
    near, far = call(sum_kernel, "sums", [single] * 2, (sums[0], *terms), moved=3 * MB)
    far = shifted(far, "yh", 1)
    gate_up_grad, down_grad = call(
        functools.partial(finish_kernel, hid),
        "finish",
        [((block, 2 * hid), BF16), ((hid, block), BF16)],
        (near, far),
        moved=MB,
    )
    n_z = lax.axis_size("z")
    z_masks = [2**k for k in range(n_z.bit_length() - 1)]
    steps = [("z", m) for m in z_masks[:2]] + [("yl", 1), ("yl", 2)]
    steps += [("z", m) for m in z_masks[2:]]
    bits = [m.bit_length() - 1 + (n_z.bit_length() - 1 if a == "yl" else 0) for a, m in steps]

    def crossed(a, axis, mask):
        return lax.ppermute(a, axis, [(i, i ^ mask) for i in range(lax.axis_size(axis))])

    for step in steps[:EARLY]:
        value = jnp.concatenate([value, crossed(value, *step)], axis=0)
    send_back = call(
        functools.partial(forward_kernel, cap),
        "forward",
        [chunk_shape],
        (got_first, gu, down),
        scratch=(chunk_shape, ((hid, model), BF16), chunk_shape, row_shape, row_shape),
        after=(*terms, value),
        hbm_in=(0, 2),
        hbm_out=(0,),
        semaphores=(groups + 1, groups),
        flops=2**31,
        moved=7 * MB,
    )
    got_back = exchange(send_back)
    for step in steps[EARLY:-1]:
        value = jnp.concatenate([value, crossed(value, *step)], axis=0)
    gate_grads = call(
        functools.partial(gate_grad_kernel, cap, n_z, bits),
        "gate_grad",
        [((1, tokens), F32)],
        (
            jnp.stack([lax.axis_index("yl"), lax.axis_index("z")]).astype(I32),
            value,
            crossed(value, *steps[-1]),
            row(routes_second),
            row(gates_second),
        ),
        scalars=1,
        moved=MB // 8,
    )
    mixed_first = call(
        functools.partial(combine_kernel, cap),
        "combine",
        [((tokens, model), BF16)],
        (got_back, mix),
        scratch=(row_shape,),
        flops=2**29,
        moved=2 * MB,
    )
    return (
        mixed_first,
        gate_grads.reshape(tokens, 1),
        gate_up_grad[None],
        down_grad[None],
    )


def solution(mesh):
    n_ep, n_dp = mesh.devices.shape
    lows = 4
    n_x = n_dp // 4
    fine = Mesh(mesh.devices.reshape(lows, n_ep // lows, 2, n_x, 2), ALL)
    tokens = P(ALL, None)
    return jax.shard_map(
        functools.partial(local, n_x),
        mesh=fine,
        in_specs=(
            tokens,
            tokens,
            tokens,
            P(EP, None, None),
            P(EP, None, None),
            P(EP, ("yh", "x", "core"), None, None),
            tokens,
            tokens,
            tokens,
        ),
        out_specs=(
            tokens,
            tokens,
            P(EP, ("yh", "x", "core"), None),
            P(EP, None, ("yh", "x", "core")),
        ),
        check_vma=False,
    )
```

```python
import functools

import jax
import jax.numpy as jnp
from jax import lax
from jax.experimental import pallas as pl
from jax.experimental.pallas import tpu as pltpu
from jax.sharding import Mesh, PartitionSpec as P

BF16 = jnp.bfloat16
F32 = jnp.float32
I32 = jnp.int32
EP = ("yl", "z")
ALL = ("yl", "z", "yh", "x", "core")
CHUNK = 8
EXTRA = 128


def iota(shape, dim):
    return lax.broadcasted_iota(I32, shape, dim)


def dot(a, b, ca=1, cb=0):
    return lax.dot_general(a, b, (((ca,), (cb,)), ((), ())), preferred_element_type=F32)


def start_copy(source, target, semaphore):
    copy = pltpu.make_async_copy(source, target, semaphore)
    copy.start()
    return copy


def group(ref, g):
    return ref.at[pl.ds(g * GROUP, GROUP)]


def slots_of(routes, experts):
    tokens = routes.shape[1]
    onehot = (iota((experts, tokens), 0) == routes).astype(F32)
    earlier = (iota((tokens, tokens), 0) < iota((tokens, tokens), 1)).astype(F32)
    before = dot(onehot.astype(BF16), earlier.astype(BF16))
    return onehot, jnp.sum(onehot * before, axis=0, keepdims=True).astype(I32)


def order_of(rows, cap, dim):
    j = iota((rows, rows), dim)
    per = rows * cap // CHUNK
    return j % CHUNK // cap * per + j // CHUNK * cap + j % cap


GROUP = 256


def from_chunks(chunks_ref, rows_ref, cap, arrivals=None):
    width = chunks_ref.shape[1]
    pieces = CHUNK // cap
    per = GROUP // pieces
    order = (iota((GROUP, GROUP), 0) == order_of(GROUP, cap, 1)).astype(F32)
    order = order.astype(BF16)
    for g in range(chunks_ref.shape[0] // GROUP):
        if arrivals:
            arrivals[g].wait()
        part = dot(order, chunks_ref[g * GROUP : (g + 1) * GROUP, :]).astype(BF16)
        for q in range(pieces):
            rows_ref[g * per : (g + 1) * per, q * width : (q + 1) * width] = part[
                q * per : (q + 1) * per
            ]


def to_chunks(rows_ref, chunks_ref, out_ref, semaphores, cap):
    width = chunks_ref.shape[1]
    pieces = CHUNK // cap
    per = GROUP // pieces
    copies = []
    order = (iota((GROUP, GROUP), 1) == order_of(GROUP, cap, 0)).astype(F32)
    order = order.astype(BF16)
    for g in range(chunks_ref.shape[0] // GROUP):
        part = jnp.concatenate(
            [
                rows_ref[g * per : (g + 1) * per, q * width : (q + 1) * width]
                for q in range(pieces)
            ],
            axis=0,
        )
        chunks_ref[g * GROUP : (g + 1) * GROUP, :] = dot(order, part).astype(BF16)
        copies.append(start_copy(group(chunks_ref, g), group(out_ref, g), semaphores.at[g]))
    for copy in copies:
        copy.wait()


def send_rows(
    experts, cap, routes, weights, tokens_ref, chunks_ref, out_ref, semaphores, arrival
):
    tokens = routes.shape[1]
    width = chunks_ref.shape[1]
    _, slots = slots_of(routes, experts)
    base = routes * CHUNK + slots
    groups, pieces = range(chunks_ref.shape[0] // GROUP), range(CHUNK // cap)
    row = iota((GROUP, tokens), 0)
    select = [
        [
            jnp.where(row == base + (q * cap - g * GROUP), weights, 0.0).astype(BF16)
            for q in pieces
        ]
        for g in groups
    ]
    copies = []
    arrival.wait()
    for g in groups:
        total = None
        for q in pieces:
            term = dot(select[g][q], tokens_ref[:, q * width : (q + 1) * width])
            total = term if total is None else total + term
        chunks_ref[g * GROUP : (g + 1) * GROUP, :] = total.astype(BF16)
        copies.append(start_copy(group(chunks_ref, g), group(out_ref, g), semaphores.at[g]))
    return slots, copies


def dispatch_second_kernel(
    experts,
    cap,
    routes_hbm,
    gates_hbm,
    tokens_hbm,
    out_ref,
    routes_ref,
    gates_ref,
    tokens_ref,
    chunks_ref,
    in_semaphores,
    out_semaphores,
):
    pairs = ((routes_hbm, routes_ref), (gates_hbm, gates_ref), (tokens_hbm, tokens_ref))
    first, second, third = [
        start_copy(a, b, in_semaphores.at[k]) for k, (a, b) in enumerate(pairs)
    ]
    first.wait()
    second.wait()
    _, copies = send_rows(
        experts,
        cap,
        routes_ref[...],
        gates_ref[...].astype(F32),
        tokens_ref,
        chunks_ref,
        out_ref,
        out_semaphores,
        third,
    )
    for copy in copies:
        copy.wait()


def dispatch_first_kernel(
    experts,
    cap,
    routes_ref,
    gates_ref,
    other_routes_ref,
    tokens_hbm,
    out_ref,
    mix_ref,
    pick_ref,
    tokens_ref,
    chunks_ref,
    in_semaphores,
    out_semaphores,
):
    arrival = start_copy(tokens_hbm, tokens_ref, in_semaphores.at[0])
    routes = routes_ref[...]
    slots, copies = send_rows(
        experts,
        cap,
        routes,
        jnp.ones(routes.shape, F32),
        tokens_ref,
        chunks_ref,
        out_ref,
        out_semaphores,
        arrival,
    )
    place = iota((experts * cap, routes.shape[1]), 0)
    hit = place == routes * cap + slots
    mix_ref[...] = jnp.where(hit, gates_ref[...].astype(F32), 0.0).T.astype(BF16)
    routes = other_routes_ref[...]
    _, slots = slots_of(routes, experts)
    pick_ref[...] = (place == routes * cap + slots).astype(F32).T.astype(BF16)
    for copy in copies:
        copy.wait()


def saved_kernel(x_ref, gu_ref, act_ref, gate_ref, up_ref):
    hid = act_ref.shape[1]
    both = dot(x_ref[...], gu_ref[...])
    gate, up = both[:, :hid], both[:, hid:]
    squash = jax.nn.sigmoid(gate)
    swish = gate * squash
    act_ref[...] = (swish * up).astype(BF16)
    gate_ref[...] = up * squash * (1.0 + gate * (1.0 - squash))
    up_ref[...] = swish


def backward_kernel(
    cap,
    at_ref,
    chunks_ref,
    down_ref,
    x_ref,
    act_ref,
    gate_ref,
    up_ref,
    keep_ref,
    send_ref,
    value_ref,
    rows_ref,
    both_ref,
):
    hid = act_ref.shape[1]
    block = keep_ref.shape[1]
    core, y, x = at_ref[0], at_ref[1], at_ref[2]
    from_chunks(chunks_ref, rows_ref, cap)
    scaled = dot(rows_ref[...], down_ref[...], 1, 1)
    value = jnp.sum(scaled * act_ref[...].astype(F32), axis=1, keepdims=True)
    lane = iota(value_ref.shape, 1)
    parts = jnp.zeros(value_ref.shape, F32)
    for k in range(3):
        part = value.astype(BF16).astype(F32)
        parts = jnp.where(lane == k, part, parts)
        value = value - part
    value_ref[...] = parts.astype(BF16)
    both_ref[:, :hid] = (scaled * gate_ref[...]).astype(BF16)
    both_ref[:, hid:] = (scaled * up_ref[...]).astype(BF16)
    n_x = keep_ref.shape[0] // 2
    for out_ref, other in ((send_ref, 1), (keep_ref, 0)):
        for n in range(2 * n_x):
            to = ((y + n % 2) % 2 * n_x + (x + n // 2) % n_x) * 2 + (core + other) % 2
            columns = pl.ds(pl.multiple_of(to * block, block), block)
            out_ref[n, :, : 2 * hid] = dot(x_ref[:, columns], both_ref[...], 0, 0).astype(BF16)
            out_ref[n, :, 2 * hid :] = dot(rows_ref[:, columns], act_ref[...], 0, 0).astype(BF16)


def forward_kernel(cap, chunks_hbm, gu_ref, down_hbm, value_ref, *refs):
    out_ref, chunks_ref, down_ref, back_ref, in_rows_ref, out_rows_ref = refs[-8:-2]
    in_semaphores, out_semaphores = refs[-2:]
    groups = chunks_ref.shape[0] // GROUP
    arrivals = [
        start_copy(group(chunks_hbm, g), group(chunks_ref, g), in_semaphores.at[g])
        for g in range(groups)
    ]
    down_arrival = start_copy(down_hbm, down_ref, in_semaphores.at[groups])
    model, hid = down_ref.shape[1], down_ref.shape[0]
    from_chunks(chunks_ref, in_rows_ref, cap, arrivals)
    both = dot(in_rows_ref[...], gu_ref[...])
    act = (jax.nn.silu(both[:, :hid]) * both[:, hid:]).astype(BF16)
    width = chunks_ref.shape[1]
    down_arrival.wait()
    for q in range(model // width):
        at = q * (width + EXTRA)
        out_rows_ref[:, at : at + width] = dot(
            act, down_ref[:, q * width : (q + 1) * width]
        ).astype(BF16)
        out_rows_ref[:, at + width : at + width + EXTRA] = value_ref[...]
    to_chunks(out_rows_ref, back_ref, out_ref, out_semaphores, cap)


def combine_kernel(
    cap,
    chunks_ref,
    mix_ref,
    pick_ref,
    gates_ref,
    out_hbm,
    grads_ref,
    rows_ref,
    out_ref,
    semaphores,
):
    from_chunks(chunks_ref, rows_ref, cap)
    width = chunks_ref.shape[1] - EXTRA
    copies = []
    for q in range(CHUNK // cap):
        at = q * (width + EXTRA)
        out_ref[q] = dot(mix_ref[...], rows_ref[:, at : at + width]).astype(BF16)
        target = out_hbm.at[:, pl.ds(q * width, width)]
        copies.append(start_copy(out_ref.at[q], target, semaphores.at[q]))
    value = dot(pick_ref[...], rows_ref[:, width : width + EXTRA])
    value = jnp.sum(value.T, axis=0, keepdims=True)
    grads_ref[...] = value / gates_ref[...].astype(F32)
    for copy in copies:
        copy.wait()


def pair_kernel(a_ref, b_ref, *out_refs):
    for k, out_ref in enumerate(out_refs):
        total = a_ref[2 * k : 2 * k + 2].astype(F32) + b_ref[2 * k : 2 * k + 2].astype(F32)
        out_ref[...] = total.astype(BF16)


def sum_kernel(*refs):
    *terms, near_ref, far_ref = refs
    for k, out_ref in ((1, far_ref), (0, near_ref)):
        total = terms[0][k].astype(F32)
        for term in terms[1:]:
            total = total + term[k].astype(F32)
        out_ref[...] = total.astype(BF16)


def finish_kernel(hid, a_ref, b_ref, gu_ref, down_ref):
    total = a_ref[...].astype(F32) + b_ref[...].astype(F32)
    gu_ref[...] = total[:, : 2 * hid].astype(BF16)
    down_ref[...] = total[:, 2 * hid :].T.astype(BF16)


VMEM = pl.BlockSpec(memory_space=pltpu.VMEM)
SMEM = pl.BlockSpec(memory_space=pltpu.SMEM)
ANY = pl.BlockSpec(memory_space=pl.ANY)
HBM = pl.BlockSpec(memory_space=pltpu.HBM)


def call(
    kernel,
    name,
    outs,
    args,
    scratch=(),
    scalars=0,
    after=(),
    hbm_in=(),
    hbm_out=(),
    semaphores=(),
    limit=16,
    flops=0,
    moved=0,
):
    shapes = [
        pltpu.HBM(*o) if k in hbm_out else jax.ShapeDtypeStruct(*o) for k, o in enumerate(outs)
    ]
    args = [
        pltpu.with_memory_space_constraint(a, pltpu.HBM) if k in hbm_in else a
        for k, a in enumerate(args)
    ]
    spaces = [SMEM if k < scalars else HBM if k in hbm_in else VMEM for k in range(len(args))]
    result = pl.pallas_call(
        kernel,
        name=name,
        out_shape=shapes,
        in_specs=spaces + [ANY] * len(after),
        out_specs=[HBM if k in hbm_out else VMEM for k in range(len(outs))],
        scratch_shapes=[pltpu.VMEM(*s) for s in scratch]
        + [pltpu.SemaphoreType.DMA((n,)) for n in semaphores],
        compiler_params=pltpu.CompilerParams(vmem_limit_bytes=limit * 2**20),
        cost_estimate=pl.CostEstimate(flops=flops, bytes_accessed=moved, transcendentals=0),
    )(*args, *after)
    return result[0] if len(outs) == 1 else result


def local(
    n_x,
    tokens_first,
    routes_first,
    gates_first,
    gate_up_weight,
    down_weight,
    saved_inputs,
    upstream,
    routes_second,
    gates_second,
):
    experts = lax.axis_size("yl") * lax.axis_size("z")
    places, model = saved_inputs.shape[2:]
    cap = places // experts
    tokens = tokens_first.shape[0]
    width = model * cap // CHUNK
    gu, down, x = gate_up_weight[0], down_weight[0], saved_inputs[0, 0]
    hid = down.shape[0]
    block = model // (4 * n_x)
    MB = 2**20
    groups = experts * CHUNK // GROUP

    def row(a):
        return a.reshape(1, tokens)

    def exchange(chunks):
        wide = chunks.shape[1]
        chunks = chunks.reshape(experts, CHUNK, wide)
        moved = lax.all_to_all(chunks, EP, split_axis=0, concat_axis=0, tiled=True)
        return moved.reshape(experts * CHUNK, wide)

    def shifted(a, axis, k):
        size = lax.axis_size(axis)
        return lax.ppermute(a, axis, [(i, (i + k) % size) for i in range(size)])

    chunk_shape = ((experts * CHUNK, width), BF16)
    back_shape = ((experts * CHUNK, width + EXTRA), BF16)
    row_shape = ((places, model), BF16)
    back_rows = ((places, model + CHUNK // cap * EXTRA), BF16)
    extra_shape = ((places, EXTRA), BF16)
    pick_shape = ((tokens, places), BF16)
    here = jnp.stack(
        [lax.axis_index("core"), lax.axis_index("yh"), lax.axis_index("x")]
    ).astype(I32)

    send_second = call(
        functools.partial(dispatch_second_kernel, experts, cap),
        "dispatch_second",
        [chunk_shape],
        (row(routes_second), row(gates_second), upstream),
        scratch=(
            ((1, tokens), I32),
            ((1, tokens), BF16),
            ((tokens, model), BF16),
            chunk_shape,
        ),
        hbm_in=(0, 1, 2),
        hbm_out=(0,),
        semaphores=(3, groups),
        flops=2**29,
        moved=2 * MB,
    )
    got_second = exchange(send_second)
    send_first, mix, pick = call(
        functools.partial(dispatch_first_kernel, experts, cap),
        "dispatch_first",
        [chunk_shape, pick_shape, pick_shape],
        (row(routes_first), row(gates_first), row(routes_second), tokens_first),
        scratch=(((tokens, model), BF16), chunk_shape),
        hbm_in=(3,),
        hbm_out=(0,),
        semaphores=(1, groups),
        flops=2**29,
        moved=2 * MB,
    )
    act, by_gate, by_up = call(
        saved_kernel,
        "saved",
        [((places, hid), BF16), ((places, hid), F32), ((places, hid), F32)],
        (x, gu),
        flops=2**30,
        moved=6 * MB,
    )
    got_first = exchange(send_first)

    half = ((2 * n_x, block, 3 * hid), BF16)
    keep, send, value = call(
        functools.partial(backward_kernel, cap),
        "backward",
        [half, half, extra_shape],
        (here, got_second, down, x, act, by_gate, by_up),
        scratch=(row_shape, ((places, 2 * hid), BF16)),
        scalars=1,
        flops=2**31,
        moved=12 * MB,
    )
    other = shifted(send, "core", 1)
    pair = ((2, block, 3 * hid), BF16)
    sums = call(pair_kernel, "pairs", [pair] * n_x, (keep, other), moved=8 * MB)
    order = sorted(range(1, n_x), key=lambda k: -min(k, n_x - k))
    terms = [shifted(sums[k], "x", k) for k in order]
    single = ((block, 3 * hid), BF16)
    near, far = call(sum_kernel, "sums", [single] * 2, (sums[0], *terms), moved=3 * MB)
    far = shifted(far, "yh", 1)
    gate_up_grad, down_grad = call(
        functools.partial(finish_kernel, hid),
        "finish",
        [((block, 2 * hid), BF16), ((hid, block), BF16)],
        (near, far),
        moved=MB,
    )
    send_back = call(
        functools.partial(forward_kernel, cap),
        "forward",
        [back_shape],
        (got_first, gu, down, value),
        scratch=(chunk_shape, ((hid, model), BF16), back_shape, row_shape, back_rows),
        after=tuple(terms),
        hbm_in=(0, 2),
        hbm_out=(0,),
        semaphores=(groups + 1, groups),
        flops=2**31,
        moved=7 * MB,
    )
    got_back = exchange(send_back)
    mixed_first, gate_grads = call(
        functools.partial(combine_kernel, cap),
        "combine",
        [((tokens, model), BF16), ((1, tokens), F32)],
        (got_back, mix, pick, row(gates_second)),
        scratch=(back_rows, ((CHUNK // cap, tokens, width), BF16)),
        hbm_out=(0,),
        semaphores=(CHUNK // cap,),
        flops=2**29,
        moved=2 * MB,
    )
    return (
        mixed_first,
        gate_grads.reshape(tokens, 1),
        gate_up_grad[None],
        down_grad[None],
    )


def solution(mesh):
    n_ep, n_dp = mesh.devices.shape
    lows = 4
    n_x = n_dp // 4
    fine = Mesh(mesh.devices.reshape(lows, n_ep // lows, 2, n_x, 2), ALL)
    tokens = P(ALL, None)
    return jax.shard_map(
        functools.partial(local, n_x),
        mesh=fine,
        in_specs=(
            tokens,
            tokens,
            tokens,
            P(EP, None, None),
            P(EP, None, None),
            P(EP, ("yh", "x", "core"), None, None),
            tokens,
            tokens,
            tokens,
        ),
        out_specs=(
            tokens,
            tokens,
            P(EP, ("yh", "x", "core"), None),
            P(EP, None, ("yh", "x", "core")),
        ),
        check_vma=False,
    )
```

```python
import functools

import jax
import jax.numpy as jnp
from jax import lax
from jax.experimental import pallas as pl
from jax.experimental.pallas import tpu as pltpu
from jax.sharding import Mesh, PartitionSpec as P

BF16 = jnp.bfloat16
F32 = jnp.float32
I32 = jnp.int32
EP = ("yl", "z")
ALL = ("yl", "z", "yh", "x", "core")
CHUNK = 8
EXTRA = 128


def iota(shape, dim):
    return lax.broadcasted_iota(I32, shape, dim)


def dot(a, b, ca=1, cb=0):
    return lax.dot_general(a, b, (((ca,), (cb,)), ((), ())), preferred_element_type=F32)


def start_copy(source, target, semaphore):
    copy = pltpu.make_async_copy(source, target, semaphore)
    copy.start()
    return copy


def group(ref, g):
    return ref.at[pl.ds(g * GROUP, GROUP)]


def slots_of(routes, experts):
    tokens = routes.shape[1]
    onehot = (iota((experts, tokens), 0) == routes).astype(F32)
    earlier = (iota((tokens, tokens), 0) < iota((tokens, tokens), 1)).astype(F32)
    before = dot(onehot.astype(BF16), earlier.astype(BF16))
    return onehot, jnp.sum(onehot * before, axis=0, keepdims=True).astype(I32)


def order_of(rows, cap, dim):
    j = iota((rows, rows), dim)
    per = rows * cap // CHUNK
    return j % CHUNK // cap * per + j // CHUNK * cap + j % cap


GROUP = 256


def from_chunks(chunks_ref, rows_ref, cap, arrivals=None):
    width = chunks_ref.shape[1]
    pieces = CHUNK // cap
    per = GROUP // pieces
    order = (iota((GROUP, GROUP), 0) == order_of(GROUP, cap, 1)).astype(F32)
    order = order.astype(BF16)
    for g in range(chunks_ref.shape[0] // GROUP):
        if arrivals:
            arrivals[g].wait()
        part = dot(order, chunks_ref[g * GROUP : (g + 1) * GROUP, :]).astype(BF16)
        for q in range(pieces):
            rows_ref[g * per : (g + 1) * per, q * width : (q + 1) * width] = part[
                q * per : (q + 1) * per
            ]


def to_chunks(rows_ref, chunks_ref, out_ref, semaphores, cap):
    width = chunks_ref.shape[1]
    pieces = CHUNK // cap
    per = GROUP // pieces
    copies = []
    order = (iota((GROUP, GROUP), 1) == order_of(GROUP, cap, 0)).astype(F32)
    order = order.astype(BF16)
    for g in range(chunks_ref.shape[0] // GROUP):
        part = jnp.concatenate(
            [
                rows_ref[g * per : (g + 1) * per, q * width : (q + 1) * width]
                for q in range(pieces)
            ],
            axis=0,
        )
        chunks_ref[g * GROUP : (g + 1) * GROUP, :] = dot(order, part).astype(BF16)
        copies.append(start_copy(group(chunks_ref, g), group(out_ref, g), semaphores.at[g]))
    for copy in copies:
        copy.wait()


def send_rows(
    experts, cap, routes, weights, tokens_ref, chunks_ref, out_ref, semaphores, arrival
):
    tokens = routes.shape[1]
    width = chunks_ref.shape[1]
    _, slots = slots_of(routes, experts)
    base = routes * CHUNK + slots
    copies = []
    arrival.wait()
    for g in range(chunks_ref.shape[0] // GROUP):
        row = iota((GROUP, tokens), 0) + g * GROUP
        total = None
        for q in range(CHUNK // cap):
            select = jnp.where(row == base + q * cap, weights, 0.0).astype(BF16)
            term = dot(select, tokens_ref[:, q * width : (q + 1) * width])
            total = term if total is None else total + term
        chunks_ref[g * GROUP : (g + 1) * GROUP, :] = total.astype(BF16)
        copies.append(start_copy(group(chunks_ref, g), group(out_ref, g), semaphores.at[g]))
    return slots, copies


def dispatch_second_kernel(
    experts,
    cap,
    routes_hbm,
    gates_hbm,
    tokens_hbm,
    out_ref,
    routes_ref,
    gates_ref,
    tokens_ref,
    chunks_ref,
    in_semaphores,
    out_semaphores,
):
    pairs = ((routes_hbm, routes_ref), (gates_hbm, gates_ref), (tokens_hbm, tokens_ref))
    first, second, third = [
        start_copy(a, b, in_semaphores.at[k]) for k, (a, b) in enumerate(pairs)
    ]
    first.wait()
    second.wait()
    _, copies = send_rows(
        experts,
        cap,
        routes_ref[...],
        gates_ref[...].astype(F32),
        tokens_ref,
        chunks_ref,
        out_ref,
        out_semaphores,
        third,
    )
    for copy in copies:
        copy.wait()


def dispatch_first_kernel(
    experts,
    cap,
    routes_ref,
    gates_ref,
    other_routes_ref,
    tokens_hbm,
    out_ref,
    mix_ref,
    pick_ref,
    tokens_ref,
    chunks_ref,
    in_semaphores,
    out_semaphores,
):
    arrival = start_copy(tokens_hbm, tokens_ref, in_semaphores.at[0])
    routes = routes_ref[...]
    slots, copies = send_rows(
        experts,
        cap,
        routes,
        jnp.ones(routes.shape, F32),
        tokens_ref,
        chunks_ref,
        out_ref,
        out_semaphores,
        arrival,
    )
    place = iota((experts * cap, routes.shape[1]), 0)
    hit = place == routes * cap + slots
    mix_ref[...] = jnp.where(hit, gates_ref[...].astype(F32), 0.0).T.astype(BF16)
    routes = other_routes_ref[...]
    _, slots = slots_of(routes, experts)
    pick_ref[...] = (place == routes * cap + slots).astype(F32).T.astype(BF16)
    for copy in copies:
        copy.wait()


def saved_kernel(x_ref, gu_ref, act_ref, gate_ref, up_ref):
    hid = act_ref.shape[1]
    both = dot(x_ref[...], gu_ref[...])
    gate, up = both[:, :hid], both[:, hid:]
    squash = jax.nn.sigmoid(gate)
    swish = gate * squash
    act_ref[...] = (swish * up).astype(BF16)
    gate_ref[...] = up * squash * (1.0 + gate * (1.0 - squash))
    up_ref[...] = swish


def backward_kernel(
    cap,
    at_ref,
    chunks_ref,
    down_ref,
    x_ref,
    act_ref,
    gate_ref,
    up_ref,
    keep_ref,
    send_ref,
    value_ref,
    rows_ref,
    both_ref,
):
    hid = act_ref.shape[1]
    block = keep_ref.shape[1]
    core, y, x = at_ref[0], at_ref[1], at_ref[2]
    from_chunks(chunks_ref, rows_ref, cap)
    scaled = dot(rows_ref[...], down_ref[...], 1, 1)
    value = jnp.sum(scaled * act_ref[...].astype(F32), axis=1, keepdims=True)
    lane = iota(value_ref.shape, 1)
    parts = jnp.zeros(value_ref.shape, F32)
    for k in range(3):
        part = value.astype(BF16).astype(F32)
        parts = jnp.where(lane == k, part, parts)
        value = value - part
    value_ref[...] = parts.astype(BF16)
    both_ref[:, :hid] = (scaled * gate_ref[...]).astype(BF16)
    both_ref[:, hid:] = (scaled * up_ref[...]).astype(BF16)
    n_x = keep_ref.shape[0] // 2
    for out_ref, other in ((send_ref, 1), (keep_ref, 0)):
        for n in range(2 * n_x):
            to = ((y + n % 2) % 2 * n_x + (x + n // 2) % n_x) * 2 + (core + other) % 2
            columns = pl.ds(pl.multiple_of(to * block, block), block)
            out_ref[n, :, : 2 * hid] = dot(x_ref[:, columns], both_ref[...], 0, 0).astype(BF16)
            out_ref[n, :, 2 * hid :] = dot(rows_ref[:, columns], act_ref[...], 0, 0).astype(BF16)


def forward_kernel(cap, chunks_hbm, gu_ref, down_hbm, value_ref, *refs):
    out_ref, chunks_ref, down_ref, back_ref, in_rows_ref, out_rows_ref = refs[-8:-2]
    in_semaphores, out_semaphores = refs[-2:]
    groups = chunks_ref.shape[0] // GROUP
    arrivals = [
        start_copy(group(chunks_hbm, g), group(chunks_ref, g), in_semaphores.at[g])
        for g in range(groups)
    ]
    down_arrival = start_copy(down_hbm, down_ref, in_semaphores.at[groups])
    model, hid = down_ref.shape[1], down_ref.shape[0]
    from_chunks(chunks_ref, in_rows_ref, cap, arrivals)
    both = dot(in_rows_ref[...], gu_ref[...])
    act = (jax.nn.silu(both[:, :hid]) * both[:, hid:]).astype(BF16)
    down_arrival.wait()
    out_rows_ref[:, :model] = dot(act, down_ref[...]).astype(BF16)
    out_rows_ref[:, model:] = value_ref[...]
    half = back_ref.shape[0] // 2
    copies = []
    for g in range(2):
        part = out_rows_ref[g * half * cap : (g + 1) * half * cap, :]
        back_ref[g * half : (g + 1) * half] = part.reshape(half, cap, part.shape[1])
        piece = pl.ds(g * half, half)
        copies.append(start_copy(back_ref.at[piece], out_ref.at[piece], out_semaphores.at[g]))
    for copy in copies:
        copy.wait()


def combine_kernel(
    cap, chunks_ref, mix_ref, pick_ref, gates_ref, out_ref, grads_ref, rows_ref
):
    rows_ref[...] = chunks_ref[...].reshape(rows_ref.shape)
    model = out_ref.shape[1]
    out_ref[...] = dot(mix_ref[...], rows_ref[:, :model]).astype(BF16)
    value = dot(pick_ref[...], rows_ref[:, model:])
    value = jnp.sum(value.T, axis=0, keepdims=True)
    grads_ref[...] = value / gates_ref[...].astype(F32)


def pair_kernel(a_ref, b_ref, *out_refs):
    for k, out_ref in enumerate(out_refs):
        total = a_ref[2 * k : 2 * k + 2].astype(F32) + b_ref[2 * k : 2 * k + 2].astype(F32)
        out_ref[...] = total.astype(BF16)


def sum_kernel(*refs):
    *terms, near_ref, far_ref = refs
    for k, out_ref in ((1, far_ref), (0, near_ref)):
        total = terms[0][k].astype(F32)
        for term in terms[1:]:
            total = total + term[k].astype(F32)
        out_ref[...] = total.astype(BF16)


def finish_kernel(hid, a_ref, b_ref, gu_ref, down_ref):
    total = a_ref[...].astype(F32) + b_ref[...].astype(F32)
    gu_ref[...] = total[:, : 2 * hid].astype(BF16)
    down_ref[...] = total[:, 2 * hid :].T.astype(BF16)


VMEM = pl.BlockSpec(memory_space=pltpu.VMEM)
SMEM = pl.BlockSpec(memory_space=pltpu.SMEM)
ANY = pl.BlockSpec(memory_space=pl.ANY)
HBM = pl.BlockSpec(memory_space=pltpu.HBM)


def call(
    kernel,
    name,
    outs,
    args,
    scratch=(),
    scalars=0,
    after=(),
    hbm_in=(),
    hbm_out=(),
    semaphores=(),
    limit=16,
    flops=0,
    moved=0,
):
    shapes = [
        pltpu.HBM(*o) if k in hbm_out else jax.ShapeDtypeStruct(*o) for k, o in enumerate(outs)
    ]
    args = [
        pltpu.with_memory_space_constraint(a, pltpu.HBM) if k in hbm_in else a
        for k, a in enumerate(args)
    ]
    spaces = [SMEM if k < scalars else HBM if k in hbm_in else VMEM for k in range(len(args))]
    result = pl.pallas_call(
        kernel,
        name=name,
        out_shape=shapes,
        in_specs=spaces + [ANY] * len(after),
        out_specs=[HBM if k in hbm_out else VMEM for k in range(len(outs))],
        scratch_shapes=[pltpu.VMEM(*s) for s in scratch]
        + [pltpu.SemaphoreType.DMA((n,)) for n in semaphores],
        compiler_params=pltpu.CompilerParams(vmem_limit_bytes=limit * 2**20),
        cost_estimate=pl.CostEstimate(flops=flops, bytes_accessed=moved, transcendentals=0),
    )(*args, *after)
    return result[0] if len(outs) == 1 else result


def local(
    n_x,
    tokens_first,
    routes_first,
    gates_first,
    gate_up_weight,
    down_weight,
    saved_inputs,
    upstream,
    routes_second,
    gates_second,
):
    experts = lax.axis_size("yl") * lax.axis_size("z")
    places, model = saved_inputs.shape[2:]
    cap = places // experts
    tokens = tokens_first.shape[0]
    width = model * cap // CHUNK
    gu, down, x = gate_up_weight[0], down_weight[0], saved_inputs[0, 0]
    hid = down.shape[0]
    block = model // (4 * n_x)
    MB = 2**20
    groups = experts * CHUNK // GROUP

    def row(a):
        return a.reshape(1, tokens)

    def exchange(chunks):
        wide = chunks.shape[1]
        chunks = chunks.reshape(experts, CHUNK, wide)
        moved = lax.all_to_all(chunks, EP, split_axis=0, concat_axis=0, tiled=True)
        return moved.reshape(experts * CHUNK, wide)

    def shifted(a, axis, k):
        size = lax.axis_size(axis)
        return lax.ppermute(a, axis, [(i, (i + k) % size) for i in range(size)])

    chunk_shape = ((experts * CHUNK, width), BF16)
    back_shape = ((experts, cap, model + EXTRA), BF16)
    row_shape = ((places, model), BF16)
    back_rows = ((places, model + EXTRA), BF16)
    extra_shape = ((places, EXTRA), BF16)
    pick_shape = ((tokens, places), BF16)
    here = jnp.stack(
        [lax.axis_index("core"), lax.axis_index("yh"), lax.axis_index("x")]
    ).astype(I32)

    send_second = call(
        functools.partial(dispatch_second_kernel, experts, cap),
        "dispatch_second",
        [chunk_shape],
        (row(routes_second), row(gates_second), upstream),
        scratch=(
            ((1, tokens), I32),
            ((1, tokens), BF16),
            ((tokens, model), BF16),
            chunk_shape,
        ),
        hbm_in=(0, 1, 2),
        hbm_out=(0,),
        semaphores=(3, groups),
        flops=2**29,
        moved=2 * MB,
    )
    got_second = exchange(send_second)
    send_first, mix, pick = call(
        functools.partial(dispatch_first_kernel, experts, cap),
        "dispatch_first",
        [chunk_shape, pick_shape, pick_shape],
        (row(routes_first), row(gates_first), row(routes_second), tokens_first),
        scratch=(((tokens, model), BF16), chunk_shape),
        hbm_in=(3,),
        hbm_out=(0,),
        semaphores=(1, groups),
        flops=2**29,
        moved=2 * MB,
    )
    act, by_gate, by_up = call(
        saved_kernel,
        "saved",
        [((places, hid), BF16), ((places, hid), F32), ((places, hid), F32)],
        (x, gu),
        flops=2**30,
        moved=6 * MB,
    )
    got_first = exchange(send_first)

    half = ((2 * n_x, block, 3 * hid), BF16)
    keep, send, value = call(
        functools.partial(backward_kernel, cap),
        "backward",
        [half, half, extra_shape],
        (here, got_second, down, x, act, by_gate, by_up),
        scratch=(row_shape, ((places, 2 * hid), BF16)),
        scalars=1,
        flops=2**31,
        moved=12 * MB,
    )
    other = shifted(send, "core", 1)
    pair = ((2, block, 3 * hid), BF16)
    sums = call(pair_kernel, "pairs", [pair] * n_x, (keep, other), moved=8 * MB)
    order = sorted(range(1, n_x), key=lambda k: -min(k, n_x - k))
    terms = [shifted(sums[k], "x", k) for k in order]
    single = ((block, 3 * hid), BF16)
    near, far = call(sum_kernel, "sums", [single] * 2, (sums[0], *terms), moved=3 * MB)
    far = shifted(far, "yh", 1)
    gate_up_grad, down_grad = call(
        functools.partial(finish_kernel, hid),
        "finish",
        [((block, 2 * hid), BF16), ((hid, block), BF16)],
        (near, far),
        moved=MB,
    )
    send_back = call(
        functools.partial(forward_kernel, cap),
        "forward",
        [back_shape],
        (got_first, gu, down, value),
        scratch=(chunk_shape, ((hid, model), BF16), back_shape, row_shape, back_rows),
        after=tuple(terms),
        hbm_in=(0, 2),
        hbm_out=(0,),
        semaphores=(groups + 1, 2),
        flops=2**31,
        moved=7 * MB,
    )
    got_back = lax.all_to_all(send_back, EP, split_axis=0, concat_axis=0, tiled=True)
    mixed_first, gate_grads = call(
        functools.partial(combine_kernel, cap),
        "combine",
        [((tokens, model), BF16), ((1, tokens), F32)],
        (got_back, mix, pick, row(gates_second)),
        scratch=(back_rows,),
        flops=2**29,
        moved=2 * MB,
    )
    return (
        mixed_first,
        gate_grads.reshape(tokens, 1),
        gate_up_grad[None],
        down_grad[None],
    )


def solution(mesh):
    n_ep, n_dp = mesh.devices.shape
    lows = 4
    n_x = n_dp // 4
    fine = Mesh(mesh.devices.reshape(lows, n_ep // lows, 2, n_x, 2), ALL)
    tokens = P(ALL, None)
    return jax.shard_map(
        functools.partial(local, n_x),
        mesh=fine,
        in_specs=(
            tokens,
            tokens,
            tokens,
            P(EP, None, None),
            P(EP, None, None),
            P(EP, ("yh", "x", "core"), None, None),
            tokens,
            tokens,
            tokens,
        ),
        out_specs=(
            tokens,
            tokens,
            P(EP, ("yh", "x", "core"), None),
            P(EP, None, ("yh", "x", "core")),
        ),
        check_vma=False,
    )
```
